32 devices in a mesh: seq: 4 (over y, core), head: 8 (over z, x).
Axes of the slice: x: 2, y: 2, z: 4, core: 2. Of those that a mesh axis runs over, the one named last changes fastest.
Arguments:
- gen_ids: int32 [4, 16], replicated, may hold values from 0 to 8191
- embed_rows: bfloat16 [8192, 8192], P('head', 'seq'), may hold values from -6 to 6
- w_query: bfloat16 [8192, 8192], P('seq', 'head'), may hold values from -0.0625 to 0.0625
- w_key: bfloat16 [8192, 8192], P('seq', 'head'), may hold values from -0.0625 to 0.0625
- w_value: bfloat16 [8192, 8192], P('seq', 'head'), may hold values from -0.0625 to 0.0625
- w_out: bfloat16 [8192, 8192], P('head', 'seq'), may hold values from -0.0625 to 0.0625
- prompt_keys: bfloat16 [2048, 8192], P('seq', 'head'), may hold values from -420 to 420
- prompt_values: bfloat16 [2048, 8192], P('seq', 'head'), may hold values from -6 to 6
Outputs:
- attn_out: bfloat16 [64, 8192], P('seq', 'head')
The draws below stay inside these ranges and needn't reach their ends.
All inputs are finite; a program needn't handle non-finite values.
Results may differ from the reference program's by a relative error of at most 0.034.
Values may be sent and summed in bfloat16 or wider, within the bound.
No kernel may reach another device: no remote copies, remote signals or barrier semaphores. Data moves between devices by JAX's collectives and lax.ppermute only.
A program may use at most 128 MiB of HBM per device.

```python
import math
import jax
import jax.numpy as jnp
from jax import lax

D = 8192
H = 64
HD = 128
VOCAB = 8192
S = 16
C = 4
P_SIZE = 2048


def draw_prompt_keys(key, part):
    key = jax.random.fold_in(key, 7)
    base_key = jax.random.fold_in(key, 0)
    entries = jax.random.normal(base_key, (P_SIZE, H * HD), jnp.float32)
    return entries.astype(jnp.bfloat16)


def with_ends(values, stream_key, low, high):
    index_at = [jax.random.randint(jax.random.fold_in(stream_key, axis), (), 0, length) for axis, length in enumerate(values.shape)]
    longest = values.shape.index(max(values.shape))
    neighbour = index_at[:longest] + [(index_at[longest] + 1) % values.shape[longest]] + index_at[longest + 1:]
    return values.at[tuple(index_at)].set(low).at[tuple(neighbour)].set(high)


def level_of(stream_key, extent, cuts, least, high):
    factor_of, own = 1.0, jax.random.fold_in(stream_key, 6)
    for position, parts in cuts:
        heights = jnp.exp(jax.random.uniform(jax.random.fold_in(own, position), (parts,), jnp.float32, least / len(cuts), high / len(cuts)))
        factor_of = factor_of * jnp.repeat(heights, extent[position] // parts).reshape([-1 if axis == position else 1 for axis in range(len(extent))])
    return factor_of


def bell_draw(key, extent, deviation, reach, cuts=(), held_as=jnp.bfloat16):
    result = deviation * jax.random.normal(key, extent, jnp.float32)
    if cuts:
        result = result * level_of(key, extent, cuts, -0.22, 0.18)
    return jnp.clip(result, -reach, reach).astype(held_as)


def setup_inputs(seed: int = 0) -> dict:
    key_of = jax.random.split(jax.random.key(seed), 9)
    gen_ids = with_ends(jax.random.randint(key_of[0], (C, S), 0, VOCAB), jax.random.fold_in(key_of[0], 1), 0, VOCAB - 1).astype(jnp.int32)
    embed_rows = bell_draw(key_of[1], (VOCAB, D), 1.0, 6.0, ((0, 8), (1, 4)))
    w_query = bell_draw(key_of[2], (D, H * HD), D ** -0.5, 0.0625, ((0, 4), (1, 8)))
    w_key = bell_draw(key_of[3], (D, H * HD), D ** -0.5, 0.0625, ((0, 4), (1, 8)))
    w_value = bell_draw(key_of[4], (D, H * HD), D ** -0.5, 0.0625, ((0, 4), (1, 8)))
    w_out = bell_draw(key_of[5], (H * HD, D), (H * HD) ** -0.5, 0.0625, ((0, 8), (1, 4)))
    prompt_keys = draw_prompt_keys(jax.random.fold_in(key_of[8], 71), 0)
    prompt_values = bell_draw(key_of[7], (P_SIZE, H * HD), 1.0, 6.0, ((0, 4), (1, 8)))
    return dict(gen_ids=gen_ids, embed_rows=embed_rows, w_query=w_query, w_key=w_key, w_value=w_value, w_out=w_out, prompt_keys=prompt_keys, prompt_values=prompt_values)


def rotate(vectors, positions):
    half_size = vectors.shape[-1] // 2
    frequency = 10000.0 ** (-jnp.arange(half_size, dtype=jnp.float32) / half_size)
    angles = positions.astype(jnp.float32)[:, None] * frequency[None, :]
    cosine = jnp.cos(angles)[:, None, :]
    sine_part = jnp.sin(angles)[:, None, :]
    former = vectors[..., :half_size]
    latter = vectors[..., half_size:]
    return jnp.concatenate([former * cosine - latter * sine_part, former * sine_part + latter * cosine], axis=-1)

def reference(gen_ids, embed_rows, w_query, w_key, w_value, w_out, prompt_keys, prompt_values):
    cand_count, step_count = gen_ids.shape
    prompt_rows = prompt_keys.shape[0]
    embedded = embed_rows[gen_ids.reshape(-1)]
    positions = prompt_rows + jnp.arange(step_count, dtype=jnp.int32)

    def project(weight):
        return jnp.dot(embedded, weight, preferred_element_type=jnp.float32).reshape(cand_count, step_count, H, HD)
    queries = rotate(project(w_query), positions).astype(jnp.bfloat16)
    gen_keys = rotate(project(w_key), positions).astype(jnp.bfloat16)
    gen_values = project(w_value).astype(jnp.bfloat16)
    score_scale = 1.0 / math.sqrt(HD)
    causal = jnp.arange(step_count)[None, :] <= jnp.arange(step_count)[:, None]

    def one_head(packed):
        head_query, head_key, head_value, prompt_key, prompt_value = packed
        query_float = head_query.astype(jnp.float32)
        prompt_scores = jnp.einsum('csd,pd->csp', query_float, prompt_key.astype(jnp.float32)) * score_scale
        own_scores = jnp.einsum('csd,ctd->cst', query_float, head_key.astype(jnp.float32)) * score_scale
        own_scores = jnp.where(causal[None], own_scores, -jnp.inf)
        peak = jnp.maximum(lax.optimization_barrier(jnp.max(prompt_scores, axis=-1)), lax.optimization_barrier(jnp.max(own_scores, axis=-1)))
        prompt_weights = jnp.exp(prompt_scores - peak[..., None])
        own_weights = jnp.exp(own_scores - peak[..., None])
        weight_sum = lax.optimization_barrier(jnp.sum(prompt_weights, axis=-1)) + lax.optimization_barrier(jnp.sum(own_weights, axis=-1))
        prompt_rounded = lax.optimization_barrier(prompt_weights.astype(jnp.bfloat16)).astype(jnp.float32)
        own_rounded = lax.optimization_barrier(own_weights.astype(jnp.bfloat16)).astype(jnp.float32)
        accumulated = jnp.einsum('csp,pd->csd', prompt_rounded, prompt_value.astype(jnp.float32))
        accumulated = accumulated + jnp.einsum('cst,ctd->csd', own_rounded, head_value.astype(jnp.float32))
        return (accumulated / weight_sum[..., None]).astype(jnp.bfloat16)
    stacked_keys = prompt_keys.reshape(prompt_rows, H, HD).transpose(1, 0, 2)
    stacked_values = prompt_values.reshape(prompt_rows, H, HD).transpose(1, 0, 2)
    per_head = lax.map(one_head, (queries.transpose(2, 0, 1, 3), gen_keys.transpose(2, 0, 1, 3), gen_values.transpose(2, 0, 1, 3), stacked_keys, stacked_values))
    attended = per_head.transpose(1, 2, 0, 3).reshape(cand_count * step_count, H * HD)
    return jnp.dot(attended, w_out, preferred_element_type=jnp.float32).astype(jnp.bfloat16)
```

```python
import math

import jax
import jax.numpy as jnp
from jax import lax
from jax.experimental import pallas as pl
from jax.experimental.pallas import tpu as pltpu
from jax.sharding import PartitionSpec as P

HD = 128
CORES = 2
MIB = 1 << 20
BF16 = jnp.bfloat16
F32 = jnp.float32


class Plan:
    def __init__(self, mesh, gen_ids, w_query, w_out, prompt_keys):
        self.seq, self.head = mesh.shape["seq"], mesh.shape["head"]
        self.cands, self.steps = gen_ids.shape
        self.tokens = self.cands * self.steps
        self.features, self.width = w_query.shape
        self.prompt_rows = prompt_keys.shape[0]
        self.inner = math.gcd(self.head, 4)
        self.outer = self.head // self.inner
        self.inner_rows = self.tokens // self.inner
        self.half = self.width // CORES
        self.chips = self.seq // CORES
        self.parts = self.head // self.seq
        self.share = self.tokens // self.seq
        self.owned = self.tokens // self.chips
        self.columns = w_out.shape[1] // self.parts

    def send(self, value, route):
        pairs = []
        for s in range(self.seq):
            for h in range(self.head):
                to_s, to_h = route(s, h)
                if (to_s, to_h) != (s, h):
                    pairs.append((s * self.head + h, to_s * self.head + to_h))
        return lax.ppermute(value, ("seq", "head"), pairs)

    def over_seq(self, value, step):
        return self.send(value, lambda s, h: (s ^ step, h))

    def over_head(self, value, step):
        return self.send(value, lambda s, h: (s, h ^ step))


VMEM_SPEC = pl.BlockSpec(memory_space=pltpu.VMEM)
ANY_SPEC = pl.BlockSpec(memory_space=pl.ANY)


def aligned(index, size):
    return pl.ds(pl.multiple_of(index * size, size), size)


def in_hbm(value):
    return pltpu.with_memory_space_constraint(value, pltpu.HBM)


def call(kernel, out_shape, in_specs, out_specs, scratch, limit, *args, cost=None):
    return pl.pallas_call(
        kernel,
        out_shape=out_shape,
        in_specs=in_specs,
        out_specs=out_specs,
        scratch_shapes=scratch,
        cost_estimate=cost,
        compiler_params=pltpu.CompilerParams(vmem_limit_bytes=limit * MIB),
    )(*args)


def pick(plan, gen_ids, embed_rows):
    vocab = embed_rows.shape[0]
    rows, inner, steps = plan.inner_rows, plan.inner, plan.steps
    cut = 2 * HD
    pieces = vocab // cut

    def kernel(ids_ref, embed_ref, *refs):
        outs, (ids, held, found, ids_sem, sems) = refs[:inner], refs[inner:]
        ids_copy = pltpu.make_async_copy(ids_ref, ids, ids_sem)
        ids_copy.start()
        copies = []
        for piece in range(pieces):
            window = pl.ds(piece * cut, cut)
            copies.append(
                pltpu.make_async_copy(embed_ref.at[window], held.at[window], sems.at[piece])
            )
            copies[-1].start()
        head_index = lax.axis_index("head")
        mine = lax.rem(head_index, inner)
        diagonal = lax.broadcasted_iota(jnp.int32, (steps, steps), 0) == (
            lax.broadcasted_iota(jnp.int32, (steps, steps), 1)
        )
        lanes = lax.broadcasted_iota(jnp.int32, (steps, vocab), 1) + head_index * vocab
        lanes = lanes.astype(F32)
        ids_copy.wait()
        selectors = []
        for block in range(inner):
            for cand in range(rows // steps):
                row = ids[pl.ds((block ^ mine) * (rows // steps) + cand, 1), :].astype(F32)
                column = jnp.sum(jnp.where(diagonal, row, 0.0), axis=1, keepdims=True)
                selectors.append((column == lanes).astype(F32).astype(BF16))
        selector = jnp.concatenate(selectors)
        for piece, copy in enumerate(copies):
            window = slice(piece * cut, (piece + 1) * cut)
            copy.wait()
            part = jnp.dot(selector[:, window], held[window, :], preferred_element_type=F32)
            if piece:
                part = part + found[...]
            if piece < pieces - 1:
                found[...] = part
        for block in range(inner):
            outs[block][...] = part[block * rows : (block + 1) * rows].astype(BF16)

    out = jax.ShapeDtypeStruct((rows, plan.features), BF16)
    return call(
        kernel,
        [out] * inner,
        [ANY_SPEC] * 2,
        [VMEM_SPEC] * inner,
        [
            pltpu.VMEM(gen_ids.shape, jnp.int32),
            pltpu.VMEM(embed_rows.shape, BF16),
            pltpu.VMEM((plan.tokens, plan.features), F32),
            pltpu.SemaphoreType.DMA,
            pltpu.SemaphoreType.DMA((pieces,)),
        ],
        16,
        in_hbm(gen_ids),
        in_hbm(embed_rows),
    )


def bring(after, source):
    def kernel(_, source_ref, out_ref, sems):
        pieces = 4
        size = source.shape[0] // pieces
        copies = [
            pltpu.make_async_copy(
                source_ref.at[pl.ds(k * size, size)], out_ref.at[pl.ds(k * size, size)], sems.at[k]
            )
            for k in range(pieces)
        ]
        for copy in copies:
            copy.start()
        for copy in copies:
            copy.wait()

    return call(
        kernel,
        jax.ShapeDtypeStruct(source.shape, source.dtype),
        [ANY_SPEC] * 2,
        ANY_SPEC,
        [pltpu.SemaphoreType.DMA((4,))],
        4,
        after,
        in_hbm(source),
    )


def gather_embedded(plan, gen_ids, embed_rows, w_key, w_value):
    picked = pick(plan, gen_ids, embed_rows)
    order = list(range(1, plan.inner))[::-1]
    total = picked[0]
    for moved in [plan.over_head(picked[step], step) for step in order]:
        total = total + moved
    w_key = bring(total, w_key)
    whole = total
    for step in range(1, plan.outer):
        whole = whole + plan.over_head(total, step * plan.inner)
    whole, w_key = lax.optimization_barrier((whole, w_key))
    w_value = bring(whole, w_value)
    return [whole] + [plan.over_head(whole, step) for step in order], w_key, w_value


def prompt_half(plan, prompt_keys, prompt_values, other, *after):
    rows, half = plan.prompt_rows, plan.half

    def kernel(keys_ref, values_ref, *refs):
        out_ref, sems = refs[-2:]
        core = lax.rem(lax.axis_index("seq"), CORES)
        window = aligned(1 - core if other else core, half)
        copies = [
            pltpu.make_async_copy(
                source.at[:, window], out_ref.at[pl.ds(place * rows, rows)], sems.at[place]
            )
            for place, source in enumerate((keys_ref, values_ref))
        ]
        for copy in copies:
            copy.start()
        for copy in copies:
            copy.wait()

    return call(
        kernel,
        jax.ShapeDtypeStruct((2 * rows, half), BF16),
        [ANY_SPEC] * (2 + len(after)),
        ANY_SPEC,
        [pltpu.SemaphoreType.DMA((2,))],
        4,
        in_hbm(prompt_keys),
        in_hbm(prompt_values),
        *after,
    )


def project_half(plan, embedded, weights, other, dtype):
    rows, half = plan.inner_rows, plan.half

    def kernel(*refs):
        blocks, sources = refs[: plan.inner], refs[plan.inner : plan.inner + 3]
        out_ref, joined = refs[plan.inner + 3 :]
        core = lax.rem(lax.axis_index("seq"), CORES)
        mine = lax.rem(lax.axis_index("head"), plan.inner)
        for place, block in enumerate(blocks):
            distance = (plan.inner - place) % plan.inner
            joined[aligned(distance ^ mine, rows), :] = block[...]
        window = aligned(1 - core if other else core, half)
        for kind in range(3):
            product = jnp.dot(
                joined[...], sources[kind][:, window], preferred_element_type=F32
            )
            out_ref[:, kind * half : (kind + 1) * half] = product.astype(dtype)

    return call(
        kernel,
        jax.ShapeDtypeStruct((plan.tokens, 3 * half), dtype),
        [VMEM_SPEC] * (plan.inner + 3),
        VMEM_SPEC,
        [pltpu.VMEM((plan.tokens, plan.features), BF16)],
        16,
        *embedded,
        *weights,
    )


def sum_cores(plan, own, received):
    tokens, half, owned = plan.tokens, plan.half, plan.owned

    def kernel(own_ref, received_ref, *refs):
        outs, total = refs[: plan.chips], refs[plan.chips]
        total[...] = own_ref[...] + received_ref[...].astype(F32)
        chip = lax.axis_index("seq") // CORES
        for dy in range(plan.chips):
            out, rows = outs[dy], aligned(chip ^ dy, owned)
            out[:tokens] = total[:, :half].astype(out.dtype)
            out[tokens : tokens + owned] = total[rows, half : 2 * half].astype(out.dtype)
            out[tokens + owned :] = total[rows, 2 * half :].astype(out.dtype)

    shape = (tokens + 2 * owned, half)
    return call(
        kernel,
        [jax.ShapeDtypeStruct(shape, BF16 if dy else F32) for dy in range(plan.chips)],
        [VMEM_SPEC] * 2,
        [VMEM_SPEC] * plan.chips,
        [pltpu.VMEM((tokens, 3 * half), F32)],
        8,
        own,
        received,
    )


def project(plan, embedded, weights):
    received = plan.over_seq(project_half(plan, embedded, weights, True, BF16), 1)
    own = project_half(plan, embedded, weights, False, F32)
    parts = sum_cores(plan, own, received)
    return [parts[0]] + [plan.over_seq(parts[dy], dy * CORES) for dy in range(1, plan.chips)]


def angle_tables(plan):
    half_size = HD // 2
    frequency = 10000.0 ** (-jnp.arange(half_size, dtype=F32) / half_size)
    positions = plan.prompt_rows * plan.seq + jnp.arange(plan.steps, dtype=jnp.int32)
    angles = positions.astype(F32)[:, None] * frequency[None, :]
    cosine, sine_part = jnp.cos(angles), jnp.sin(angles)
    return (
        jnp.concatenate([cosine, cosine], axis=-1),
        jnp.concatenate([-sine_part, sine_part], axis=-1),
    )


def attend(plan, parts, kept, swapped, tables):
    tokens, half, owned, share = plan.tokens, plan.half, plan.owned, plan.share
    rows, heads = plan.prompt_rows, plan.half // HD
    scale = 1.0 / math.sqrt(HD)
    transposed = (((1,), (1,)), ((), ()))

    def kernel(*refs):
        sums, refs = refs[: plan.chips], refs[plan.chips :]
        kept_ref, swapped_ref, cosine_ref, sine_ref = refs[:4]
        near_ref, far_ref, result = refs[4:]
        core = lax.rem(lax.axis_index("seq"), CORES)
        chip = lax.axis_index("seq") // CORES
        total = sums[0][...]
        for dy in range(1, plan.chips):
            total = total + sums[dy][...].astype(F32)
        cosine, sine_part = cosine_ref[...][None], sine_ref[...][None]

        def rotated(vectors):
            turned = pltpu.roll(vectors, HD // 2, 1)
            shaped = vectors.reshape(-1, plan.steps, HD) * cosine
            shaped = shaped + turned.reshape(-1, plan.steps, HD) * sine_part
            return shaped.reshape(vectors.shape).astype(BF16)

        row = lax.broadcasted_iota(jnp.int32, (tokens, owned), 0)
        column = lax.broadcasted_iota(jnp.int32, (tokens, owned), 1) + chip * owned
        seen = (row // plan.steps == column // plan.steps) & (column <= row)
        lane = lax.broadcasted_iota(jnp.int32, (tokens, HD), 1)
        logs = jnp.zeros((tokens, HD), F32)
        for head in range(heads):
            lanes = slice(head * HD, (head + 1) * HD)
            query = rotated(total[:tokens, lanes])
            gen_key = rotated(total[tokens : tokens + owned, lanes])
            gen_value = total[tokens + owned :, lanes].astype(BF16)

            def score(key):
                return (
                    lax.dot_general(query, key, transposed, preferred_element_type=F32) * scale
                )

            scores = [
                score(kept_ref[:rows, lanes]),
                score(swapped_ref[:rows, lanes]),
                jnp.where(seen, score(gen_key), -jnp.inf),
            ]
            held = [kept_ref[rows:, lanes], swapped_ref[rows:, lanes], gen_value]
            peak = jnp.max(scores[0], axis=1, keepdims=True)
            for part in scores[1:]:
                peak = jnp.maximum(peak, jnp.max(part, axis=1, keepdims=True))
            weight_sum, summed = 0.0, 0.0
            for part, value in zip(scores, held):
                weight = jnp.exp(part - peak)
                weight_sum = weight_sum + jnp.sum(weight, axis=1, keepdims=True)
                summed = summed + jnp.dot(
                    weight.astype(BF16), value, preferred_element_type=F32
                )
            result[:, lanes] = (summed / weight_sum).astype(BF16)
            rest = peak + jnp.log(weight_sum)
            for term in range(3):
                piece = rest.astype(BF16).astype(F32)
                rest = rest - piece
                logs = jnp.where(lane == 3 * head + term, piece, logs)
        result[:, half:] = logs.astype(BF16)
        for pair in range(plan.chips):
            place = pl.ds(pair * share, share)
            near_ref[place, :] = result[aligned(pair * CORES + core, share), :]
            far_ref[place, :] = result[aligned(pair * CORES + 1 - core, share), :]

    out = jax.ShapeDtypeStruct((tokens // CORES, half + HD), BF16)
    near, far = call(
        kernel,
        [out] * 2,
        [VMEM_SPEC] * (plan.chips + 4),
        [VMEM_SPEC] * 2,
        [pltpu.VMEM((tokens, half + HD), BF16)],
        24,
        *parts,
        kept,
        swapped,
        *tables,
    )
    got = {k: plan.over_seq(far if k % CORES else near, k) for k in range(1, plan.seq)}
    return [near] + [got[k] for k in range(1, plan.seq)]


def multiply_out(plan, attended, own, swapped):
    half, columns = plan.half, plan.columns
    rows = plan.tokens // CORES
    keys = [(dq, dx) for dq in range(CORES) for dx in range(plan.parts)]

    def kernel(*refs):
        parts, refs = refs[: plan.seq], refs[plan.seq :]
        (own_ref, swapped_ref), refs = refs[:2], refs[2:]
        outs, (joined,) = dict(zip(keys, refs)), refs[len(keys) :]
        core = lax.rem(lax.axis_index("seq"), CORES)
        head_index = lax.axis_index("head")
        part_index = lax.rem(head_index, plan.parts)
        block = lax.rem(head_index // plan.parts, CORES)
        for side in range(CORES):
            sources = [parts[step] for step in range(side, plan.seq, CORES)]
            first = (core ^ side) * half
            for head in range(half // HD):
                lanes = slice(head * HD, (head + 1) * HD)
                logs = [
                    sum(
                        source[:, half + 3 * head + term : half + 3 * head + term + 1].astype(F32)
                        for term in (2, 1, 0)
                    )
                    for source in sources
                ]
                top = logs[0]
                for one in logs[1:]:
                    top = jnp.maximum(top, one)
                scales = [jnp.exp(one - top) for one in logs]
                mixed = sum(f * source[:, lanes].astype(F32) for f, source in zip(scales, sources))
                mixed = (mixed / sum(scales)).astype(BF16)
                joined[:, pl.ds(pl.multiple_of(first + head * HD, HD), HD)] = mixed
        left = joined[...]

        def multiply(*weights):
            for dq, dx in keys[::-1]:
                weight = weights[dq][:, aligned(part_index ^ dx, columns)]
                product = jnp.dot(left, weight, preferred_element_type=F32)
                outs[dq, dx][...] = product.astype(outs[dq, dx].dtype)

        @pl.when(block == core)
        def _():
            multiply(own_ref, swapped_ref)

        @pl.when(block != core)
        def _():
            multiply(swapped_ref, own_ref)

    shape = (rows, columns)
    made = call(
        kernel,
        [jax.ShapeDtypeStruct(shape, BF16 if any(key) else F32) for key in keys],
        [VMEM_SPEC] * (plan.seq + 2),
        [VMEM_SPEC] * len(keys),
        [pltpu.VMEM((rows, plan.width), BF16)],
        24,
        *attended,
        own,
        swapped,
    )
    got = [
        plan.send(value, lambda s, h: (s, h ^ (dq * plan.parts + dx)))
        for (dq, dx), value in list(zip(keys, made))[:0:-1]
    ]
    return [made[0]] + got


def sum_parts(plan, got):
    shape = (plan.share, plan.columns)

    def kernel(*refs):
        ins, outs, held = refs[: len(got)], refs[len(got) : -1], refs[-1]
        total = ins[0][...]
        for ref in ins[1:]:
            total = total + ref[...].astype(F32)
        held[...] = total
        group = lax.axis_index("head") // (plan.parts * CORES)
        for step in range(plan.chips):
            outs[step][...] = held[aligned(group ^ step, plan.share), :].astype(BF16)

    made = call(
        kernel,
        [jax.ShapeDtypeStruct(shape, BF16)] * plan.chips,
        [VMEM_SPEC] * len(got),
        [VMEM_SPEC] * plan.chips,
        [pltpu.VMEM((plan.chips * plan.share, plan.columns), F32)],
        16,
        *got,
    )
    size = plan.parts * CORES

    def moved(step):
        def route(s, h):
            return (h // size ^ step) * CORES + s % CORES, s // CORES * size + h % size

        return plan.send(made[step], route)

    def last(own_ref, *refs):
        chip, group = lax.axis_index("seq") // CORES, lax.axis_index("head") // size
        total = jnp.zeros(shape, F32)
        for ref in refs[:-1]:
            total = total + ref[...].astype(F32)
        total = total + jnp.where(chip == group, own_ref[...].astype(F32), 0.0)
        refs[-1][...] = total.astype(BF16)

    return call(
        last,
        jax.ShapeDtypeStruct(shape, BF16),
        [VMEM_SPEC] * (plan.chips + 1),
        VMEM_SPEC,
        [],
        8,
        made[0],
        *[moved(step) for step in range(plan.chips)],
    )


def solution(mesh):
    def body(gen_ids, embed_rows, w_query, w_key, w_value, w_out, prompt_keys, prompt_values):
        plan = Plan(mesh, gen_ids, w_query, w_out, prompt_keys)
        embedded, w_key, w_value = gather_embedded(plan, gen_ids, embed_rows, w_key, w_value)
        swapped_out = plan.over_seq(w_out, 1)
        swapped = plan.over_seq(prompt_half(plan, prompt_keys, prompt_values, True), 1)
        parts = project(plan, embedded, (w_query, w_key, w_value))
        kept = prompt_half(plan, prompt_keys, prompt_values, False, parts[0])
        attended = attend(plan, parts, kept, swapped, angle_tables(plan))
        return sum_parts(plan, multiply_out(plan, attended, w_out, swapped_out))

    return jax.shard_map(
        body,
        mesh=mesh,
        in_specs=(
            P(),
            P("head", "seq"),
            P("seq", "head"),
            P("seq", "head"),
            P("seq", "head"),
            P("head", "seq"),
            P("seq", "head"),
            P("seq", "head"),
        ),
        out_specs=P("seq", "head"),
        check_vma=False,
    )
```

```python
import math

import jax
import jax.numpy as jnp
from jax import lax
from jax.experimental import pallas as pl
from jax.experimental.pallas import tpu as pltpu
from jax.sharding import PartitionSpec as P

HD = 128
CORES = 2
MIB = 1 << 20
BF16 = jnp.bfloat16
F32 = jnp.float32


class Plan:
    def __init__(self, mesh, gen_ids, w_query, w_out, prompt_keys):
        self.seq, self.head = mesh.shape["seq"], mesh.shape["head"]
        self.cands, self.steps = gen_ids.shape
        self.tokens = self.cands * self.steps
        self.features, self.width = w_query.shape
        self.prompt_rows = prompt_keys.shape[0]
        self.inner = math.gcd(self.head, 4)
        self.outer = self.head // self.inner
        self.room = -(-2 * self.tokens // (self.head * 16)) * 16
        self.half = self.width // CORES
        self.chips = self.seq // CORES
        self.parts = self.head // self.seq
        self.share = self.tokens // self.seq
        self.owned = self.tokens // self.chips
        self.columns = w_out.shape[1] // self.parts

    def send(self, value, route):
        pairs = []
        for s in range(self.seq):
            for h in range(self.head):
                to_s, to_h = route(s, h)
                pairs.append((s * self.head + h, to_s * self.head + to_h))
        return lax.ppermute(value, ("seq", "head"), pairs)

    def over_seq(self, value, step):
        return self.send(value, lambda s, h: (s ^ step, h))

    def over_head(self, value, step):
        return self.send(value, lambda s, h: (s, h ^ step))


VMEM_SPEC = pl.BlockSpec(memory_space=pltpu.VMEM)
ANY_SPEC = pl.BlockSpec(memory_space=pl.ANY)


def aligned(index, size):
    return pl.ds(pl.multiple_of(index * size, size), size)


def in_hbm(value):
    return pltpu.with_memory_space_constraint(value, pltpu.HBM)


def call(kernel, out_shape, in_specs, out_specs, scratch, limit, *args, cost=None):
    return pl.pallas_call(
        kernel,
        out_shape=out_shape,
        in_specs=in_specs,
        out_specs=out_specs,
        scratch_shapes=scratch,
        cost_estimate=cost,
        compiler_params=pltpu.CompilerParams(vmem_limit_bytes=limit * MIB),
    )(*args)


def iota(shape, axis):
    return lax.broadcasted_iota(jnp.int32, shape, axis)


def id_columns(plan, ids):
    steps = plan.steps
    corner = iota((steps, steps), 0) == iota((steps, steps), 1)
    columns = []
    for cand in range(plan.cands):
        row = ids[cand : cand + 1, :].astype(F32)
        columns.append(jnp.sum(jnp.where(corner, row, 0.0), axis=1, keepdims=True))
    return jnp.concatenate(columns)


def pick(plan, gen_ids, embed_rows):
    vocab = embed_rows.shape[0]
    tokens, room = plan.tokens, plan.room
    cut = 2 * HD
    pieces = vocab // cut

    def kernel(ids_ref, embed_ref, rows_ref, ids, held, found, ids_sem, sems):
        ids_copy = pltpu.make_async_copy(ids_ref, ids, ids_sem)
        ids_copy.start()
        copies = []
        for piece in range(pieces):
            window = pl.ds(piece * cut, cut)
            copies.append(
                pltpu.make_async_copy(embed_ref.at[window], held.at[window], sems.at[piece])
            )
            copies[-1].start()
        base = (lax.axis_index("head") * vocab).astype(F32)
        first, second = iota((tokens, tokens), 0), iota((tokens, tokens), 1)
        ids_copy.wait()
        column = id_columns(plan, ids) - base
        local = (column >= 0) & (column < vocab)
        row = jnp.sum(jnp.where(first == second, column, 0.0), axis=0, keepdims=True)
        earlier = jnp.where((first < second) & local, 1.0, 0.0)
        rank = jnp.sum(earlier, axis=0, keepdims=True)
        wanted = (row >= 0) & (row < vocab) & (rank == iota((room, tokens), 0).astype(F32))
        chosen = jnp.sum(jnp.where(wanted, row + 1.0, 0.0), axis=1, keepdims=True) - 1.0
        selector = (chosen == iota((room, vocab), 1).astype(F32)).astype(F32).astype(BF16)
        for piece, copy in enumerate(copies):
            window = slice(piece * cut, (piece + 1) * cut)
            copy.wait()
            part = jnp.dot(selector[:, window], held[window, :], preferred_element_type=F32)
            if piece:
                part = part + found[...]
            if piece < pieces - 1:
                found[...] = part
        rows_ref[...] = part.astype(BF16)

    return call(
        kernel,
        jax.ShapeDtypeStruct((room, plan.features), BF16),
        [ANY_SPEC] * 2,
        VMEM_SPEC,
        [
            pltpu.VMEM(gen_ids.shape, jnp.int32),
            pltpu.VMEM(embed_rows.shape, BF16),
            pltpu.VMEM((room, plan.features), F32),
            pltpu.SemaphoreType.DMA,
            pltpu.SemaphoreType.DMA((pieces,)),
        ],
        16,
        in_hbm(gen_ids),
        in_hbm(embed_rows),
    )


def find_places(plan, after, gen_ids, vocab):
    tokens, room = plan.tokens, plan.room
    slots = plan.head * room

    def kernel(_, ids_ref, places_ref, beyond_ref, ids, ids_sem):
        ids_copy = pltpu.make_async_copy(ids_ref, ids, ids_sem)
        ids_copy.start()
        ids_copy.wait()
        owner = id_columns(plan, ids).astype(jnp.int32) // vocab
        member = (owner == iota((tokens, HD), 1)).astype(F32).astype(BF16)
        same = lax.dot_general(
            member, member, (((1,), (1,)), ((), ())), preferred_element_type=F32
        )
        earlier = iota((tokens, tokens), 1) < iota((tokens, tokens), 0)
        rank = jnp.sum(jnp.where(earlier, same, 0.0), axis=1, keepdims=True)
        beyond = jnp.sum(jnp.where(rank >= room, 1.0, 0.0), axis=0, keepdims=True)
        beyond_ref[...] = jnp.broadcast_to(beyond, beyond_ref.shape)
        slot = iota((tokens, slots), 1)
        place = slot // (plan.outer * room)
        group = lax.rem(slot // room, plan.outer)
        distance = lax.rem(plan.inner - place, plan.inner) + group * plan.inner
        filled = (owner == (lax.axis_index("head") ^ distance)) & (
            rank == lax.rem(slot, room).astype(F32)
        )
        places_ref[...] = filled.astype(F32).astype(BF16)

    return call(
        kernel,
        [
            jax.ShapeDtypeStruct((tokens, slots), BF16),
            jax.ShapeDtypeStruct((8, HD), F32),
        ],
        [ANY_SPEC] * 2,
        [VMEM_SPEC] * 2,
        [pltpu.VMEM(gen_ids.shape, jnp.int32), pltpu.SemaphoreType.DMA],
        8,
        after,
        in_hbm(gen_ids),
    )


def rows_beyond(plan, gen_ids, embed_rows):
    vocab = embed_rows.shape[0]
    ids = gen_ids.reshape(-1)
    owner = ids // vocab
    order = jnp.arange(plan.tokens)
    rank = jnp.sum((owner[:, None] == owner[None]) & (order[None] < order[:, None]), axis=1)
    shifted = jnp.where(rank >= plan.room, ids - lax.axis_index("head") * vocab, -1)
    selector = (shifted[:, None] == jnp.arange(vocab, dtype=jnp.int32)[None]).astype(BF16)

    def kernel(selector_ref, embed_ref, out_ref, held, sem):
        copy = pltpu.make_async_copy(embed_ref, held, sem)
        copy.start()
        copy.wait()
        found = jnp.dot(selector_ref[...], held[...], preferred_element_type=F32)
        out_ref[...] = found.astype(BF16)

    picked = call(
        kernel,
        jax.ShapeDtypeStruct((plan.tokens, plan.features), BF16),
        [VMEM_SPEC, ANY_SPEC],
        VMEM_SPEC,
        [pltpu.VMEM(embed_rows.shape, BF16), pltpu.SemaphoreType.DMA],
        16,
        selector,
        in_hbm(embed_rows),
    )
    step = 1
    while step < plan.head:
        picked = picked + plan.over_head(picked, step)
        step *= 2
    return picked


def bring(after, source):
    def kernel(_, source_ref, out_ref, sems):
        pieces = 4
        size = source.shape[0] // pieces
        copies = [
            pltpu.make_async_copy(
                source_ref.at[pl.ds(k * size, size)], out_ref.at[pl.ds(k * size, size)], sems.at[k]
            )
            for k in range(pieces)
        ]
        for copy in copies:
            copy.start()
        for copy in copies:
            copy.wait()

    return call(
        kernel,
        jax.ShapeDtypeStruct(source.shape, source.dtype),
        [ANY_SPEC] * 2,
        ANY_SPEC,
        [pltpu.SemaphoreType.DMA((4,))],
        4,
        after,
        in_hbm(source),
    )


def prompt_to_swap(plan, after, prompt_keys, prompt_values):
    half = plan.half

    def kernel(_, keys_ref, values_ref, given_keys_ref, given_values_ref, sems):
        window = aligned(1 - lax.rem(lax.axis_index("seq"), CORES), half)
        copies = [
            pltpu.make_async_copy(keys_ref.at[:, window], given_keys_ref, sems.at[0]),
            pltpu.make_async_copy(values_ref.at[:, window], given_values_ref, sems.at[1]),
        ]
        for copy in copies:
            copy.start()
        for copy in copies:
            copy.wait()

    return call(
        kernel,
        [jax.ShapeDtypeStruct((plan.prompt_rows, half), BF16)] * 2,
        [ANY_SPEC] * 3,
        [ANY_SPEC] * 2,
        [pltpu.SemaphoreType.DMA((2,))],
        4,
        after,
        in_hbm(prompt_keys),
        in_hbm(prompt_values),
    )


def gather_embedded(
    plan, gen_ids, embed_rows, w_key, w_value, prompt_keys, prompt_values, w_out
):
    rows = pick(plan, gen_ids, embed_rows)
    places, beyond = find_places(plan, rows, gen_ids, embed_rows.shape[0])
    rest = lax.cond(
        beyond[0, 0] > 0.5,
        lambda: rows_beyond(plan, gen_ids, embed_rows),
        lambda: jnp.zeros((plan.tokens, plan.features), BF16),
    )
    w_key = bring(rest, w_key)
    across = [plan.over_head(rows, step * plan.inner) for step in range(1, plan.outer)]
    near = jnp.concatenate([rows, *across])
    near, w_key, w_out = lax.optimization_barrier((near, w_key, w_out))
    swapped_out = plan.over_seq(w_out, 1)
    given = prompt_to_swap(plan, near, prompt_keys, prompt_values)
    w_value = bring(near, w_value)
    blocks = [near] + [plan.over_head(near, step) for step in range(1, plan.inner)[::-1]]
    size = plan.outer * plan.room

    def kernel(places_ref, beyond_ref, rest_ref, *refs):
        blocks, (out_ref, held, added, sem) = refs[: plan.inner], refs[plan.inner :]
        for block, ref in enumerate(blocks):
            held[block * size : (block + 1) * size] = ref[...]
        placed = jnp.dot(places_ref[...], held[...], preferred_element_type=F32)
        out_ref[...] = placed.astype(BF16)

        @pl.when(jnp.max(beyond_ref[...]) > 0.5)
        def _():
            copy = pltpu.make_async_copy(rest_ref, added, sem)
            copy.start()
            copy.wait()
            out_ref[...] = out_ref[...] + added[...]

    embedded = call(
        kernel,
        jax.ShapeDtypeStruct((plan.tokens, plan.features), BF16),
        [VMEM_SPEC] * 2 + [ANY_SPEC] + [VMEM_SPEC] * plan.inner,
        VMEM_SPEC,
        [
            pltpu.VMEM((plan.inner * size, plan.features), BF16),
            pltpu.VMEM((plan.tokens, plan.features), BF16),
            pltpu.SemaphoreType.DMA,
        ],
        16,
        places,
        beyond,
        rest,
        *blocks,
    )
    return embedded, w_key, w_value, given, swapped_out


def prompt_half(plan, prompt_keys, prompt_values, after):
    rows, half = plan.prompt_rows, plan.half

    def kernel(_, keys_ref, values_ref, out_ref, sems):
        window = aligned(lax.rem(lax.axis_index("seq"), CORES), half)
        copies = [
            pltpu.make_async_copy(
                source.at[:, window], out_ref.at[pl.ds(place * rows, rows)], sems.at[place]
            )
            for place, source in enumerate((keys_ref, values_ref))
        ]
        for copy in copies:
            copy.start()
        for copy in copies:
            copy.wait()

    return call(
        kernel,
        jax.ShapeDtypeStruct((2 * rows, half), BF16),
        [ANY_SPEC] * 3,
        ANY_SPEC,
        [pltpu.SemaphoreType.DMA((2,))],
        4,
        after,
        in_hbm(prompt_keys),
        in_hbm(prompt_values),
    )


def project_half(plan, embedded, weights, other, dtype):
    half = plan.half

    def kernel(rows_ref, *refs):
        sources, out_ref = refs[:3], refs[3]
        core = lax.rem(lax.axis_index("seq"), CORES)
        window = aligned(1 - core if other else core, half)
        for kind in range(3):
            product = jnp.dot(
                rows_ref[...], sources[kind][:, window], preferred_element_type=F32
            )
            out_ref[:, kind * half : (kind + 1) * half] = product.astype(dtype)

    return call(
        kernel,
        jax.ShapeDtypeStruct((plan.tokens, 3 * half), dtype),
        [VMEM_SPEC] * 4,
        VMEM_SPEC,
        [],
        16,
        embedded,
        *weights,
    )


def sum_cores(plan, own, received):
    tokens, half, owned = plan.tokens, plan.half, plan.owned

    def kernel(own_ref, received_ref, *refs):
        outs, total = refs[: plan.chips], refs[plan.chips]
        total[...] = own_ref[...] + received_ref[...].astype(F32)
        chip = lax.axis_index("seq") // CORES
        for dy in range(plan.chips):
            out, rows = outs[dy], aligned(chip ^ dy, owned)
            out[:tokens] = total[:, :half].astype(out.dtype)
            out[tokens : tokens + owned] = total[rows, half : 2 * half].astype(out.dtype)
            out[tokens + owned :] = total[rows, 2 * half :].astype(out.dtype)

    shape = (tokens + 2 * owned, half)
    return call(
        kernel,
        [jax.ShapeDtypeStruct(shape, BF16 if dy else F32) for dy in range(plan.chips)],
        [VMEM_SPEC] * 2,
        [VMEM_SPEC] * plan.chips,
        [pltpu.VMEM((tokens, 3 * half), F32)],
        8,
        own,
        received,
    )


def project(plan, embedded, weights):
    received = plan.over_seq(project_half(plan, embedded, weights, True, BF16), 1)
    own = project_half(plan, embedded, weights, False, F32)
    parts = sum_cores(plan, own, received)
    return [parts[0]] + [plan.over_seq(parts[dy], dy * CORES) for dy in range(1, plan.chips)]


def angle_tables(plan):
    half_size = HD // 2
    frequency = 10000.0 ** (-jnp.arange(half_size, dtype=F32) / half_size)
    positions = plan.prompt_rows * plan.seq + jnp.arange(plan.steps, dtype=jnp.int32)
    angles = positions.astype(F32)[:, None] * frequency[None, :]
    cosine, sine_part = jnp.cos(angles), jnp.sin(angles)
    return (
        jnp.concatenate([cosine, cosine], axis=-1),
        jnp.concatenate([-sine_part, sine_part], axis=-1),
    )


def attend(plan, parts, kept, swapped, tables):
    tokens, half, owned, share = plan.tokens, plan.half, plan.owned, plan.share
    rows = plan.prompt_rows
    scale = 1.0 / math.sqrt(HD)
    transposed = (((1,), (1,)), ((), ()))

    def kernel(*refs):
        sums, refs = refs[: plan.chips], refs[plan.chips :]
        kept_ref, keys_ref, values_ref, cosine_ref, sine_ref = refs[:5]
        near_ref, far_ref, result = refs[5:]
        core = lax.rem(lax.axis_index("seq"), CORES)
        chip = lax.axis_index("seq") // CORES
        total = sums[0][...]
        for dy in range(1, plan.chips):
            total = total + sums[dy][...].astype(F32)
        cosine, sine_part = cosine_ref[...][None], sine_ref[...][None]

        def rotated(vectors):
            turned = pltpu.roll(vectors, HD // 2, 1)
            shaped = vectors.reshape(-1, plan.steps, HD) * cosine
            shaped = shaped + turned.reshape(-1, plan.steps, HD) * sine_part
            return shaped.reshape(vectors.shape).astype(BF16)

        pair = 2 * HD
        row = lax.broadcasted_iota(jnp.int32, (2 * tokens, 2 * owned), 0)
        column = lax.broadcasted_iota(jnp.int32, (2 * tokens, 2 * owned), 1)
        same_head = row // tokens == column // owned
        row, column = lax.rem(row, tokens), lax.rem(column, owned) + chip * owned
        seen = same_head & (row // plan.steps == column // plan.steps) & (column <= row)
        lane = lax.broadcasted_iota(jnp.int32, (tokens, HD), 1)
        logs = jnp.zeros((tokens, HD), F32)
        nothing = jnp.zeros((tokens, HD), BF16)
        for start in range(0, half, pair):
            lanes = slice(start, start + pair)
            near, far = slice(start, start + HD), slice(start + HD, start + pair)
            query = jnp.concatenate(
                [
                    jnp.concatenate([rotated(total[:tokens, near]), nothing], axis=1),
                    jnp.concatenate([nothing, rotated(total[:tokens, far])], axis=1),
                ]
            )
            keys, values = slice(tokens, tokens + owned), slice(tokens + owned, None)
            gen_key = jnp.concatenate([rotated(total[keys, near]), rotated(total[keys, far])])
            gen_value = jnp.concatenate([total[values, near], total[values, far]]).astype(BF16)

            def score(vectors, key):
                return (
                    lax.dot_general(vectors, key, transposed, preferred_element_type=F32) * scale
                )

            own = score(jnp.concatenate([query[:tokens, :HD], query[tokens:, HD:]]), gen_key)
            scores = [
                score(query, kept_ref[:rows, lanes]),
                score(query, keys_ref[:, lanes]),
                jnp.where(seen, own, -jnp.inf),
            ]
            peak = jnp.max(scores[0], axis=1, keepdims=True)
            for part in scores[1:]:
                peak = jnp.maximum(peak, jnp.max(part, axis=1, keepdims=True))
            weights = [jnp.exp(part - peak) for part in scores]
            weight_sum = sum(jnp.sum(weight, axis=1, keepdims=True) for weight in weights)
            weights = [weight.astype(BF16) for weight in weights]
            summed = jnp.dot(
                weights[0], kept_ref[rows:, lanes], preferred_element_type=F32
            ) + jnp.dot(weights[1], values_ref[:, lanes], preferred_element_type=F32)
            summed = jnp.concatenate([summed[:tokens, :HD], summed[tokens:, HD:]])
            summed = summed + jnp.dot(weights[2], gen_value, preferred_element_type=F32)
            mixed = (summed / weight_sum).astype(BF16)
            result[:, near] = mixed[:tokens]
            result[:, far] = mixed[tokens:]
            both = peak + jnp.log(weight_sum)
            for place, rest in enumerate((both[:tokens], both[tokens:])):
                first = 3 * (start // HD + place)
                for term in range(3):
                    piece = rest.astype(BF16).astype(F32)
                    rest = rest - piece
                    logs = jnp.where(lane == first + term, piece, logs)
        result[:, half:] = logs.astype(BF16)
        for pair in range(plan.chips):
            place = pl.ds(pair * share, share)
            near_ref[place, :] = result[aligned(pair * CORES + core, share), :]
            far_ref[place, :] = result[aligned(pair * CORES + 1 - core, share), :]

    out = jax.ShapeDtypeStruct((tokens // CORES, half + HD), BF16)
    near, far = call(
        kernel,
        [out] * 2,
        [VMEM_SPEC] * (plan.chips + 5),
        [VMEM_SPEC] * 2,
        [pltpu.VMEM((tokens, half + HD), BF16)],
        24,
        *parts,
        kept,
        *swapped,
        *tables,
    )
    got = {k: plan.over_seq(far if k % CORES else near, k) for k in range(1, plan.seq)}
    return [near] + [got[k] for k in range(1, plan.seq)]


def multiply_out(plan, attended, own, swapped):
    share, half, columns = plan.share, plan.half, plan.columns
    rows = plan.tokens // CORES
    keys = [(dy, dx) for dx in range(plan.parts) for dy in range(plan.chips)]

    def kernel(*refs):
        parts, refs = refs[: plan.seq], refs[plan.seq :]
        (own_ref, swapped_ref), refs = refs[:2], refs[2:]
        outs, (joined, held) = refs[: len(keys)], refs[len(keys) :]
        seq_index = lax.axis_index("seq")
        chip, core = seq_index // CORES, lax.rem(seq_index, CORES)
        part_index = lax.rem(lax.axis_index("head"), plan.parts)
        for side in range(CORES):
            sources = [parts[step] for step in range(side, plan.seq, CORES)]
            first = (core ^ side) * half
            for head in range(half // HD):
                lanes = slice(head * HD, (head + 1) * HD)
                logs = [
                    sum(
                        source[:, half + 3 * head + term : half + 3 * head + term + 1].astype(F32)
                        for term in (2, 1, 0)
                    )
                    for source in sources
                ]
                top = logs[0]
                for one in logs[1:]:
                    top = jnp.maximum(top, one)
                scales = [jnp.exp(one - top) for one in logs]
                mixed = sum(f * source[:, lanes].astype(F32) for f, source in zip(scales, sources))
                mixed = (mixed / sum(scales)).astype(BF16)
                joined[:, pl.ds(pl.multiple_of(first + head * HD, HD), HD)] = mixed
        left = joined[...]
        for dx in list(range(plan.parts))[::-1]:
            lanes = aligned(part_index ^ dx, columns)
            for weight, block in ((own_ref, core), (swapped_ref, 1 - core)):
                product = jnp.dot(left, weight[:, lanes], preferred_element_type=F32)
                held[...] = product
                for dy in range(plan.chips):
                    out = outs[keys.index((dy, dx))]
                    out[block] = held[aligned(chip ^ dy, share), :].astype(out.dtype)

    shape = (CORES, share, columns)
    outs = [jax.ShapeDtypeStruct(shape, BF16 if any(key) else F32) for key in keys]
    made = call(
        kernel,
        outs,
        [VMEM_SPEC] * (plan.seq + 2),
        [VMEM_SPEC] * len(keys),
        [pltpu.VMEM((rows, plan.width), BF16), pltpu.VMEM((rows, columns), F32)],
        24,
        *attended,
        own,
        swapped,
    )
    got = {}
    for key, value in list(zip(keys, made))[::-1]:
        dy, dx = key
        if any(key):
            value = plan.send(value, lambda s, h: (s ^ (dy * CORES), h ^ dx))
        got[key] = value
    return got


def sum_parts(plan, got):
    keys = list(got)
    shape = (plan.share, plan.columns)

    def kernel(*refs):
        ins, refs = dict(zip(keys, refs)), refs[len(keys) :]
        outs, (held,) = refs[: plan.seq], refs[plan.seq :]
        chip = lax.axis_index("seq") // CORES
        place = lax.axis_index("head") // plan.parts
        for dy in range(plan.chips):
            total = ins[dy, 0][...].astype(F32)
            for dx in range(1, plan.parts):
                total = total + ins[dy, dx][...].astype(F32)
            for core in range(CORES):
                held[(chip ^ dy) * CORES + core] = total[core]
        for step in range(plan.seq):
            outs[step][...] = held[place ^ step].astype(outs[step].dtype)

    outs = [jax.ShapeDtypeStruct(shape, BF16 if step else F32) for step in range(plan.seq)]
    made = call(
        kernel,
        outs,
        [VMEM_SPEC] * len(keys),
        [VMEM_SPEC] * plan.seq,
        [pltpu.VMEM((plan.seq,) + shape, F32)],
        16,
        *got.values(),
    )
    got = [
        plan.send(made[step], lambda s, h: (s, h ^ (step * plan.parts)))
        for step in list(range(1, plan.seq))[::-1]
    ]

    def last(*refs):
        total = refs[0][...]
        for ref in refs[1:-1]:
            total = total + ref[...].astype(F32)
        refs[-1][...] = total.astype(BF16)

    return call(
        last,
        jax.ShapeDtypeStruct(shape, BF16),
        [VMEM_SPEC] * plan.seq,
        VMEM_SPEC,
        [],
        8,
        made[0],
        *got,
    )


def solution(mesh):
    def body(gen_ids, embed_rows, w_query, w_key, w_value, w_out, prompt_keys, prompt_values):
        plan = Plan(mesh, gen_ids, w_query, w_out, prompt_keys)
        embedded, w_key, w_value, given, swapped_out = gather_embedded(
            plan, gen_ids, embed_rows, w_key, w_value, prompt_keys, prompt_values, w_out
        )
        swapped = [plan.over_seq(part, 1) for part in given]
        parts = project(plan, embedded, (w_query, w_key, w_value))
        kept = prompt_half(plan, prompt_keys, prompt_values, parts[0])
        attended = attend(plan, parts, kept, swapped, angle_tables(plan))
        return sum_parts(plan, multiply_out(plan, attended, w_out, swapped_out))

    return jax.shard_map(
        body,
        mesh=mesh,
        in_specs=(
            P(),
            P("head", "seq"),
            P("seq", "head"),
            P("seq", "head"),
            P("seq", "head"),
            P("head", "seq"),
            P("seq", "head"),
            P("seq", "head"),
        ),
        out_specs=P("seq", "head"),
        check_vma=False,
    )
```

```python
import math

import jax
import jax.numpy as jnp
from jax import lax
from jax.experimental import pallas as pl
from jax.experimental.pallas import tpu as pltpu
from jax.sharding import PartitionSpec as P

HD = 128
CORES = 2
MIB = 1 << 20
BF16 = jnp.bfloat16
F32 = jnp.float32


class Plan:
    def __init__(self, mesh, gen_ids, w_query, w_out, prompt_keys):
        self.seq, self.head = mesh.shape["seq"], mesh.shape["head"]
        self.cands, self.steps = gen_ids.shape
        self.tokens = self.cands * self.steps
        self.features, self.width = w_query.shape
        self.prompt_rows = prompt_keys.shape[0]
        self.inner = math.gcd(self.head, 4)
        self.outer = self.head // self.inner
        self.room = -(-2 * self.tokens // (self.head * 16)) * 16
        self.half = self.width // CORES
        self.chips = self.seq // CORES
        self.parts = self.head // self.seq
        self.share = self.tokens // self.seq
        self.owned = self.tokens // self.chips
        self.columns = w_out.shape[1] // self.parts

    def send(self, value, route):
        pairs = []
        for s in range(self.seq):
            for h in range(self.head):
                to_s, to_h = route(s, h)
                pairs.append((s * self.head + h, to_s * self.head + to_h))
        return lax.ppermute(value, ("seq", "head"), pairs)

    def over_seq(self, value, step):
        return self.send(value, lambda s, h: (s ^ step, h))

    def over_head(self, value, step):
        return self.send(value, lambda s, h: (s, h ^ step))


VMEM_SPEC = pl.BlockSpec(memory_space=pltpu.VMEM)
ANY_SPEC = pl.BlockSpec(memory_space=pl.ANY)


def aligned(index, size):
    return pl.ds(pl.multiple_of(index * size, size), size)


def in_hbm(value):
    return pltpu.with_memory_space_constraint(value, pltpu.HBM)


def call(kernel, out_shape, in_specs, out_specs, scratch, limit, *args, cost=None):
    return pl.pallas_call(
        kernel,
        out_shape=out_shape,
        in_specs=in_specs,
        out_specs=out_specs,
        scratch_shapes=scratch,
        cost_estimate=cost,
        compiler_params=pltpu.CompilerParams(vmem_limit_bytes=limit * MIB),
    )(*args)


def pick(plan, gen_ids, embed_rows):
    vocab = embed_rows.shape[0]
    tokens, steps, room = plan.tokens, plan.steps, plan.room
    cut = 2 * HD
    pieces = vocab // cut
    slots = plan.head * room

    def iota(shape, axis):
        return lax.broadcasted_iota(jnp.int32, shape, axis)

    def kernel(ids_ref, embed_ref, rows_ref, places_ref, beyond_ref, *scratch):
        ids, held, found, ids_sem, sems = scratch
        ids_copy = pltpu.make_async_copy(ids_ref, ids, ids_sem)
        ids_copy.start()
        copies = []
        for piece in range(pieces):
            window = pl.ds(piece * cut, cut)
            copies.append(
                pltpu.make_async_copy(embed_ref.at[window], held.at[window], sems.at[piece])
            )
            copies[-1].start(priority=piece % 2)
        me = lax.axis_index("head")
        ids_copy.wait()
        corner = iota((steps, steps), 0) == iota((steps, steps), 1)
        columns = []
        for cand in range(plan.cands):
            row = ids[cand : cand + 1, :].astype(F32)
            columns.append(jnp.sum(jnp.where(corner, row, 0.0), axis=1, keepdims=True))
        id_column = jnp.concatenate(columns)
        owner_column = id_column.astype(jnp.int32) // vocab

        member = (owner_column == iota((tokens, HD), 1)).astype(F32).astype(BF16)
        same = lax.dot_general(
            member, member, (((1,), (1,)), ((), ())), preferred_element_type=F32
        )
        first, second = iota((tokens, tokens), 0), iota((tokens, tokens), 1)
        rank_column = jnp.sum(jnp.where(second < first, same, 0.0), axis=1, keepdims=True)
        rank_row = jnp.sum(jnp.where(first < second, same, 0.0), axis=0, keepdims=True)
        id_row = jnp.sum(jnp.where(first == second, id_column, 0.0), axis=0, keepdims=True)
        beyond = jnp.sum(jnp.where(rank_column >= room, 1.0, 0.0), axis=0, keepdims=True)
        beyond_ref[...] = jnp.broadcast_to(beyond, beyond_ref.shape)

        slot = iota((tokens, slots), 1)
        place = slot // (plan.outer * room)
        group = lax.rem(slot // room, plan.outer)
        distance = lax.rem(plan.inner - place, plan.inner) + group * plan.inner
        filled = (owner_column == (me ^ distance)) & (
            rank_column == lax.rem(slot, room).astype(F32)
        )
        places_ref[...] = filled.astype(F32).astype(BF16)

        local = id_row - (me * vocab).astype(F32)
        wanted = (local >= 0) & (local < vocab)
        wanted = wanted & (rank_row == iota((room, tokens), 0).astype(F32))
        chosen = jnp.sum(jnp.where(wanted, local + 1.0, 0.0), axis=1, keepdims=True) - 1.0
        selector = (chosen == iota((room, vocab), 1).astype(F32)).astype(F32).astype(BF16)
        for piece, copy in enumerate(copies):
            window = slice(piece * cut, (piece + 1) * cut)
            copy.wait()
            part = jnp.dot(selector[:, window], held[window, :], preferred_element_type=F32)
            if piece:
                part = part + found[...]
            if piece < pieces - 1:
                found[...] = part
        rows_ref[...] = part.astype(BF16)

    return call(
        kernel,
        [
            jax.ShapeDtypeStruct((room, plan.features), BF16),
            jax.ShapeDtypeStruct((tokens, slots), BF16),
            jax.ShapeDtypeStruct((8, HD), F32),
        ],
        [ANY_SPEC] * 2,
        [VMEM_SPEC] * 3,
        [
            pltpu.VMEM(gen_ids.shape, jnp.int32),
            pltpu.VMEM(embed_rows.shape, BF16),
            pltpu.VMEM((room, plan.features), F32),
            pltpu.SemaphoreType.DMA,
            pltpu.SemaphoreType.DMA((pieces,)),
        ],
        16,
        in_hbm(gen_ids),
        in_hbm(embed_rows),
    )


def rows_beyond(plan, gen_ids, embed_rows):
    vocab = embed_rows.shape[0]
    ids = gen_ids.reshape(-1)
    owner = ids // vocab
    order = jnp.arange(plan.tokens)
    rank = jnp.sum((owner[:, None] == owner[None]) & (order[None] < order[:, None]), axis=1)
    shifted = jnp.where(rank >= plan.room, ids - lax.axis_index("head") * vocab, -1)
    selector = (shifted[:, None] == jnp.arange(vocab, dtype=jnp.int32)[None]).astype(BF16)

    def kernel(selector_ref, embed_ref, out_ref, held, sem):
        copy = pltpu.make_async_copy(embed_ref, held, sem)
        copy.start()
        copy.wait()
        found = jnp.dot(selector_ref[...], held[...], preferred_element_type=F32)
        out_ref[...] = found.astype(BF16)

    picked = call(
        kernel,
        jax.ShapeDtypeStruct((plan.tokens, plan.features), BF16),
        [VMEM_SPEC, ANY_SPEC],
        VMEM_SPEC,
        [pltpu.VMEM(embed_rows.shape, BF16), pltpu.SemaphoreType.DMA],
        16,
        selector,
        in_hbm(embed_rows),
    )
    step = 1
    while step < plan.head:
        picked = picked + plan.over_head(picked, step)
        step *= 2
    return picked


def bring(after, source):
    def kernel(_, source_ref, out_ref, sems):
        pieces = 4
        size = source.shape[0] // pieces
        copies = [
            pltpu.make_async_copy(
                source_ref.at[pl.ds(k * size, size)], out_ref.at[pl.ds(k * size, size)], sems.at[k]
            )
            for k in range(pieces)
        ]
        for k, copy in enumerate(copies):
            copy.start(priority=k % 2)
        for copy in copies:
            copy.wait()

    return call(
        kernel,
        jax.ShapeDtypeStruct(source.shape, source.dtype),
        [ANY_SPEC] * 2,
        ANY_SPEC,
        [pltpu.SemaphoreType.DMA((4,))],
        4,
        after,
        in_hbm(source),
    )


def prompt_to_swap(plan, after, prompt_keys, prompt_values):
    half = plan.half

    def kernel(_, keys_ref, values_ref, given_keys_ref, given_values_ref, sems):
        window = aligned(1 - lax.rem(lax.axis_index("seq"), CORES), half)
        copies = [
            pltpu.make_async_copy(keys_ref.at[:, window], given_keys_ref, sems.at[0]),
            pltpu.make_async_copy(values_ref.at[:, window], given_values_ref, sems.at[1]),
        ]
        for copy in copies:
            copy.start()
        for copy in copies:
            copy.wait()

    return call(
        kernel,
        [jax.ShapeDtypeStruct((plan.prompt_rows, half), BF16)] * 2,
        [ANY_SPEC] * 3,
        [ANY_SPEC] * 2,
        [pltpu.SemaphoreType.DMA((2,))],
        4,
        after,
        in_hbm(prompt_keys),
        in_hbm(prompt_values),
    )


def gather_embedded(
    plan, gen_ids, embed_rows, w_key, w_value, prompt_keys, prompt_values, w_out
):
    rows, places, beyond = pick(plan, gen_ids, embed_rows)
    rest = lax.cond(
        beyond[0, 0] > 0.5,
        lambda: rows_beyond(plan, gen_ids, embed_rows),
        lambda: jnp.zeros((plan.tokens, plan.features), BF16),
    )
    w_key = bring(rest, w_key)
    across = [plan.over_head(rows, step * plan.inner) for step in range(1, plan.outer)]
    near = jnp.concatenate([rows, *across])
    near, w_key, w_out = lax.optimization_barrier((near, w_key, w_out))
    swapped_out = plan.over_seq(w_out, 1)
    given = prompt_to_swap(plan, near, prompt_keys, prompt_values)
    w_value = bring(near, w_value)
    blocks = [near] + [plan.over_head(near, step) for step in range(1, plan.inner)[::-1]]
    size = plan.outer * plan.room

    def kernel(places_ref, beyond_ref, rest_ref, *refs):
        blocks, (out_ref, held, added, sem) = refs[: plan.inner], refs[plan.inner :]
        for block, ref in enumerate(blocks):
            held[block * size : (block + 1) * size] = ref[...]
        placed = jnp.dot(places_ref[...], held[...], preferred_element_type=F32)
        out_ref[...] = placed.astype(BF16)

        @pl.when(jnp.max(beyond_ref[...]) > 0.5)
        def _():
            copy = pltpu.make_async_copy(rest_ref, added, sem)
            copy.start()
            copy.wait()
            out_ref[...] = out_ref[...] + added[...]

    embedded = call(
        kernel,
        jax.ShapeDtypeStruct((plan.tokens, plan.features), BF16),
        [VMEM_SPEC] * 2 + [ANY_SPEC] + [VMEM_SPEC] * plan.inner,
        VMEM_SPEC,
        [
            pltpu.VMEM((plan.inner * size, plan.features), BF16),
            pltpu.VMEM((plan.tokens, plan.features), BF16),
            pltpu.SemaphoreType.DMA,
        ],
        16,
        places,
        beyond,
        rest,
        *blocks,
    )
    return embedded, w_key, w_value, given, swapped_out


def prompt_half(plan, prompt_keys, prompt_values, after):
    rows, half = plan.prompt_rows, plan.half

    def kernel(_, keys_ref, values_ref, out_ref, sems):
        window = aligned(lax.rem(lax.axis_index("seq"), CORES), half)
        copies = [
            pltpu.make_async_copy(
                source.at[:, window], out_ref.at[pl.ds(place * rows, rows)], sems.at[place]
            )
            for place, source in enumerate((keys_ref, values_ref))
        ]
        for copy in copies:
            copy.start()
        for copy in copies:
            copy.wait()

    return call(
        kernel,
        jax.ShapeDtypeStruct((2 * rows, half), BF16),
        [ANY_SPEC] * 3,
        ANY_SPEC,
        [pltpu.SemaphoreType.DMA((2,))],
        4,
        after,
        in_hbm(prompt_keys),
        in_hbm(prompt_values),
    )


def project_half(plan, embedded, weights, other, dtype):
    half = plan.half

    def kernel(rows_ref, *refs):
        sources, out_ref = refs[:3], refs[3]
        core = lax.rem(lax.axis_index("seq"), CORES)
        window = aligned(1 - core if other else core, half)
        for kind in range(3):
            product = jnp.dot(
                rows_ref[...], sources[kind][:, window], preferred_element_type=F32
            )
            out_ref[:, kind * half : (kind + 1) * half] = product.astype(dtype)

    return call(
        kernel,
        jax.ShapeDtypeStruct((plan.tokens, 3 * half), dtype),
        [VMEM_SPEC] * 4,
        VMEM_SPEC,
        [],
        16,
        embedded,
        *weights,
    )


def sum_cores(plan, own, received):
    tokens, half, owned = plan.tokens, plan.half, plan.owned

    def kernel(own_ref, received_ref, *refs):
        outs, total = refs[: plan.chips], refs[plan.chips]
        total[...] = own_ref[...] + received_ref[...].astype(F32)
        chip = lax.axis_index("seq") // CORES
        for dy in range(plan.chips):
            out, rows = outs[dy], aligned(chip ^ dy, owned)
            out[:tokens] = total[:, :half].astype(out.dtype)
            out[tokens : tokens + owned] = total[rows, half : 2 * half].astype(out.dtype)
            out[tokens + owned :] = total[rows, 2 * half :].astype(out.dtype)

    shape = (tokens + 2 * owned, half)
    return call(
        kernel,
        [jax.ShapeDtypeStruct(shape, BF16 if dy else F32) for dy in range(plan.chips)],
        [VMEM_SPEC] * 2,
        [VMEM_SPEC] * plan.chips,
        [pltpu.VMEM((tokens, 3 * half), F32)],
        8,
        own,
        received,
    )


def project(plan, embedded, weights):
    received = plan.over_seq(project_half(plan, embedded, weights, True, BF16), 1)
    own = project_half(plan, embedded, weights, False, F32)
    parts = sum_cores(plan, own, received)
    return [parts[0]] + [plan.over_seq(parts[dy], dy * CORES) for dy in range(1, plan.chips)]


def angle_tables(plan):
    half_size = HD // 2
    frequency = 10000.0 ** (-jnp.arange(half_size, dtype=F32) / half_size)
    positions = plan.prompt_rows * plan.seq + jnp.arange(plan.steps, dtype=jnp.int32)
    angles = positions.astype(F32)[:, None] * frequency[None, :]
    cosine, sine_part = jnp.cos(angles), jnp.sin(angles)
    return (
        jnp.concatenate([cosine, cosine], axis=-1),
        jnp.concatenate([-sine_part, sine_part], axis=-1),
    )


def attend(plan, parts, kept, swapped, tables):
    tokens, half, owned, share = plan.tokens, plan.half, plan.owned, plan.share
    rows = plan.prompt_rows
    scale = 1.0 / math.sqrt(HD)
    transposed = (((1,), (1,)), ((), ()))

    def kernel(*refs):
        sums, refs = refs[: plan.chips], refs[plan.chips :]
        kept_ref, keys_ref, values_ref, cosine_ref, sine_ref = refs[:5]
        near_ref, far_ref, result = refs[5:]
        core = lax.rem(lax.axis_index("seq"), CORES)
        chip = lax.axis_index("seq") // CORES
        total = sums[0][...]
        for dy in range(1, plan.chips):
            total = total + sums[dy][...].astype(F32)
        cosine, sine_part = cosine_ref[...][None], sine_ref[...][None]

        def rotated(vectors):
            turned = pltpu.roll(vectors, HD // 2, 1)
            shaped = vectors.reshape(-1, plan.steps, HD) * cosine
            shaped = shaped + turned.reshape(-1, plan.steps, HD) * sine_part
            return shaped.reshape(vectors.shape).astype(BF16)

        pair = 2 * HD
        row = lax.broadcasted_iota(jnp.int32, (2 * tokens, 2 * owned), 0)
        column = lax.broadcasted_iota(jnp.int32, (2 * tokens, 2 * owned), 1)
        same_head = row // tokens == column // owned
        row, column = lax.rem(row, tokens), lax.rem(column, owned) + chip * owned
        seen = same_head & (row // plan.steps == column // plan.steps) & (column <= row)
        lane = lax.broadcasted_iota(jnp.int32, (tokens, HD), 1)
        logs = jnp.zeros((tokens, HD), F32)
        nothing = jnp.zeros((tokens, HD), BF16)
        for start in range(0, half, pair):
            lanes = slice(start, start + pair)
            near, far = slice(start, start + HD), slice(start + HD, start + pair)
            query = jnp.concatenate(
                [
                    jnp.concatenate([rotated(total[:tokens, near]), nothing], axis=1),
                    jnp.concatenate([nothing, rotated(total[:tokens, far])], axis=1),
                ]
            )
            keys, values = slice(tokens, tokens + owned), slice(tokens + owned, None)
            gen_key = jnp.concatenate([rotated(total[keys, near]), rotated(total[keys, far])])
            gen_value = jnp.concatenate([total[values, near], total[values, far]]).astype(BF16)

            def score(vectors, key):
                return (
                    lax.dot_general(vectors, key, transposed, preferred_element_type=F32) * scale
                )

            own = score(jnp.concatenate([query[:tokens, :HD], query[tokens:, HD:]]), gen_key)
            scores = [
                score(query, kept_ref[:rows, lanes]),
                score(query, keys_ref[:, lanes]),
                jnp.where(seen, own, -jnp.inf),
            ]
            peak = jnp.max(scores[0], axis=1, keepdims=True)
            for part in scores[1:]:
                peak = jnp.maximum(peak, jnp.max(part, axis=1, keepdims=True))
            weights = [jnp.exp(part - peak) for part in scores]
            weight_sum = sum(jnp.sum(weight, axis=1, keepdims=True) for weight in weights)
            weights = [weight.astype(BF16) for weight in weights]
            summed = jnp.dot(
                weights[0], kept_ref[rows:, lanes], preferred_element_type=F32
            ) + jnp.dot(weights[1], values_ref[:, lanes], preferred_element_type=F32)
            summed = jnp.concatenate([summed[:tokens, :HD], summed[tokens:, HD:]])
            summed = summed + jnp.dot(weights[2], gen_value, preferred_element_type=F32)
            mixed = (summed / weight_sum).astype(BF16)
            result[:, near] = mixed[:tokens]
            result[:, far] = mixed[tokens:]
            both = peak + jnp.log(weight_sum)
            for place, rest in enumerate((both[:tokens], both[tokens:])):
                first = 3 * (start // HD + place)
                for term in range(3):
                    piece = rest.astype(BF16).astype(F32)
                    rest = rest - piece
                    logs = jnp.where(lane == first + term, piece, logs)
        result[:, half:] = logs.astype(BF16)
        for pair in range(plan.chips):
            place = pl.ds(pair * share, share)
            near_ref[place, :] = result[aligned(pair * CORES + core, share), :]
            far_ref[place, :] = result[aligned(pair * CORES + 1 - core, share), :]

    out = jax.ShapeDtypeStruct((tokens // CORES, half + HD), BF16)
    near, far = call(
        kernel,
        [out] * 2,
        [VMEM_SPEC] * (plan.chips + 5),
        [VMEM_SPEC] * 2,
        [pltpu.VMEM((tokens, half + HD), BF16)],
        24,
        *parts,
        kept,
        *swapped,
        *tables,
    )
    got = {k: plan.over_seq(far if k % CORES else near, k) for k in range(1, plan.seq)}
    return [near] + [got[k] for k in range(1, plan.seq)]


def multiply_out(plan, attended, own, swapped):
    share, half, columns = plan.share, plan.half, plan.columns
    rows = plan.tokens // CORES
    keys = [(dy, dx) for dx in range(plan.parts) for dy in range(plan.chips)]

    def kernel(*refs):
        parts, refs = refs[: plan.seq], refs[plan.seq :]
        (own_ref, swapped_ref), refs = refs[:2], refs[2:]
        outs, (joined, held) = refs[: len(keys)], refs[len(keys) :]
        seq_index = lax.axis_index("seq")
        chip, core = seq_index // CORES, lax.rem(seq_index, CORES)
        part_index = lax.rem(lax.axis_index("head"), plan.parts)
        for side in range(CORES):
            sources = [parts[step] for step in range(side, plan.seq, CORES)]
            first = (core ^ side) * half
            for head in range(half // HD):
                lanes = slice(head * HD, (head + 1) * HD)
                logs = [
                    sum(
                        source[:, half + 3 * head + term : half + 3 * head + term + 1].astype(F32)
                        for term in (2, 1, 0)
                    )
                    for source in sources
                ]
                top = logs[0]
                for one in logs[1:]:
                    top = jnp.maximum(top, one)
                scales = [jnp.exp(one - top) for one in logs]
                mixed = sum(f * source[:, lanes].astype(F32) for f, source in zip(scales, sources))
                mixed = (mixed / sum(scales)).astype(BF16)
                joined[:, pl.ds(pl.multiple_of(first + head * HD, HD), HD)] = mixed
        left = joined[...]
        for dx in list(range(plan.parts))[::-1]:
            lanes = aligned(part_index ^ dx, columns)
            for weight, block in ((own_ref, core), (swapped_ref, 1 - core)):
                product = jnp.dot(left, weight[:, lanes], preferred_element_type=F32)
                held[...] = product
                for dy in range(plan.chips):
                    out = outs[keys.index((dy, dx))]
                    out[block] = held[aligned(chip ^ dy, share), :].astype(out.dtype)

    shape = (CORES, share, columns)
    outs = [jax.ShapeDtypeStruct(shape, BF16 if any(key) else F32) for key in keys]
    made = call(
        kernel,
        outs,
        [VMEM_SPEC] * (plan.seq + 2),
        [VMEM_SPEC] * len(keys),
        [pltpu.VMEM((rows, plan.width), BF16), pltpu.VMEM((rows, columns), F32)],
        24,
        *attended,
        own,
        swapped,
    )
    got = {}
    for key, value in list(zip(keys, made))[::-1]:
        dy, dx = key
        if any(key):
            value = plan.send(value, lambda s, h: (s ^ (dy * CORES), h ^ dx))
        got[key] = value
    return got


def sum_parts(plan, got):
    keys = list(got)
    shape = (plan.share, plan.columns)

    def kernel(*refs):
        ins, refs = dict(zip(keys, refs)), refs[len(keys) :]
        outs, (held,) = refs[: plan.seq], refs[plan.seq :]
        chip = lax.axis_index("seq") // CORES
        place = lax.axis_index("head") // plan.parts
        for dy in range(plan.chips):
            total = ins[dy, 0][...].astype(F32)
            for dx in range(1, plan.parts):
                total = total + ins[dy, dx][...].astype(F32)
            for core in range(CORES):
                held[(chip ^ dy) * CORES + core] = total[core]
        for step in range(plan.seq):
            outs[step][...] = held[place ^ step].astype(outs[step].dtype)

    outs = [jax.ShapeDtypeStruct(shape, BF16 if step else F32) for step in range(plan.seq)]
    made = call(
        kernel,
        outs,
        [VMEM_SPEC] * len(keys),
        [VMEM_SPEC] * plan.seq,
        [pltpu.VMEM((plan.seq,) + shape, F32)],
        16,
        *got.values(),
    )
    got = [
        plan.send(made[step], lambda s, h: (s, h ^ (step * plan.parts)))
        for step in list(range(1, plan.seq))[::-1]
    ]

    def last(*refs):
        total = refs[0][...]
        for ref in refs[1:-1]:
            total = total + ref[...].astype(F32)
        refs[-1][...] = total.astype(BF16)

    return call(
        last,
        jax.ShapeDtypeStruct(shape, BF16),
        [VMEM_SPEC] * plan.seq,
        VMEM_SPEC,
        [],
        8,
        made[0],
        *got,
    )


def solution(mesh):
    def body(gen_ids, embed_rows, w_query, w_key, w_value, w_out, prompt_keys, prompt_values):
        plan = Plan(mesh, gen_ids, w_query, w_out, prompt_keys)
        embedded, w_key, w_value, given, swapped_out = gather_embedded(
            plan, gen_ids, embed_rows, w_key, w_value, prompt_keys, prompt_values, w_out
        )
        swapped = [plan.over_seq(part, 1) for part in given]
        parts = project(plan, embedded, (w_query, w_key, w_value))
        kept = prompt_half(plan, prompt_keys, prompt_values, parts[0])
        attended = attend(plan, parts, kept, swapped, angle_tables(plan))
        return sum_parts(plan, multiply_out(plan, attended, w_out, swapped_out))

    return jax.shard_map(
        body,
        mesh=mesh,
        in_specs=(
            P(),
            P("head", "seq"),
            P("seq", "head"),
            P("seq", "head"),
            P("seq", "head"),
            P("head", "seq"),
            P("seq", "head"),
            P("seq", "head"),
        ),
        out_specs=P("seq", "head"),
        check_vma=False,
    )
```

```python
import math

import jax
import jax.numpy as jnp
from jax import lax
from jax.experimental import pallas as pl
from jax.experimental.pallas import tpu as pltpu
from jax.sharding import PartitionSpec as P

HD = 128
CORES = 2
MIB = 1 << 20
BF16 = jnp.bfloat16
F32 = jnp.float32


class Plan:
    def __init__(self, mesh, gen_ids, w_query, w_out, prompt_keys):
        self.seq, self.head = mesh.shape["seq"], mesh.shape["head"]
        self.cands, self.steps = gen_ids.shape
        self.tokens = self.cands * self.steps
        self.features, self.width = w_query.shape
        self.prompt_rows = prompt_keys.shape[0]
        self.inner = math.gcd(self.head, 4)
        self.outer = self.head // self.inner
        self.room = -(-2 * self.tokens // (self.head * 16)) * 16
        self.half = self.width // CORES
        self.chips = self.seq // CORES
        self.parts = self.head // self.seq
        self.share = self.tokens // self.seq
        self.owned = self.tokens // self.chips
        self.columns = w_out.shape[1] // self.parts

    def send(self, value, route):
        pairs = []
        for s in range(self.seq):
            for h in range(self.head):
                to_s, to_h = route(s, h)
                pairs.append((s * self.head + h, to_s * self.head + to_h))
        return lax.ppermute(value, ("seq", "head"), pairs)

    def over_seq(self, value, step):
        return self.send(value, lambda s, h: (s ^ step, h))

    def over_head(self, value, step):
        return self.send(value, lambda s, h: (s, h ^ step))


VMEM_SPEC = pl.BlockSpec(memory_space=pltpu.VMEM)
ANY_SPEC = pl.BlockSpec(memory_space=pl.ANY)


def aligned(index, size):
    return pl.ds(pl.multiple_of(index * size, size), size)


def in_hbm(value):
    return pltpu.with_memory_space_constraint(value, pltpu.HBM)


def call(kernel, out_shape, in_specs, out_specs, scratch, limit, *args, cost=None):
    return pl.pallas_call(
        kernel,
        out_shape=out_shape,
        in_specs=in_specs,
        out_specs=out_specs,
        scratch_shapes=scratch,
        cost_estimate=cost,
        compiler_params=pltpu.CompilerParams(vmem_limit_bytes=limit * MIB),
    )(*args)


def pick(plan, gen_ids, embed_rows):
    vocab = embed_rows.shape[0]
    tokens, steps, room = plan.tokens, plan.steps, plan.room
    cut = 2 * HD
    pieces = vocab // cut
    slots = plan.head * room

    def iota(shape, axis):
        return lax.broadcasted_iota(jnp.int32, shape, axis)

    def kernel(ids_ref, embed_ref, rows_ref, places_ref, beyond_ref, *scratch):
        ids, held, found, ids_sem, sems = scratch
        ids_copy = pltpu.make_async_copy(ids_ref, ids, ids_sem)
        ids_copy.start()
        copies = []
        for piece in range(pieces):
            window = pl.ds(piece * cut, cut)
            copies.append(
                pltpu.make_async_copy(embed_ref.at[window], held.at[window], sems.at[piece])
            )
            copies[-1].start(priority=piece % 2)
        me = lax.axis_index("head")
        ids_copy.wait()
        corner = iota((steps, steps), 0) == iota((steps, steps), 1)
        columns = []
        for cand in range(plan.cands):
            row = ids[cand : cand + 1, :].astype(F32)
            columns.append(jnp.sum(jnp.where(corner, row, 0.0), axis=1, keepdims=True))
        id_column = jnp.concatenate(columns)
        owner_column = id_column.astype(jnp.int32) // vocab

        member = (owner_column == iota((tokens, HD), 1)).astype(F32).astype(BF16)
        same = lax.dot_general(
            member, member, (((1,), (1,)), ((), ())), preferred_element_type=F32
        )
        first, second = iota((tokens, tokens), 0), iota((tokens, tokens), 1)
        rank_column = jnp.sum(jnp.where(second < first, same, 0.0), axis=1, keepdims=True)
        rank_row = jnp.sum(jnp.where(first < second, same, 0.0), axis=0, keepdims=True)
        id_row = jnp.sum(jnp.where(first == second, id_column, 0.0), axis=0, keepdims=True)
        beyond = jnp.sum(jnp.where(rank_column >= room, 1.0, 0.0), axis=0, keepdims=True)
        beyond_ref[...] = jnp.broadcast_to(beyond, beyond_ref.shape)

        slot = iota((tokens, slots), 1)
        place = slot // (plan.outer * room)
        group = lax.rem(slot // room, plan.outer)
        distance = lax.rem(plan.inner - place, plan.inner) + group * plan.inner
        filled = (owner_column == (me ^ distance)) & (
            rank_column == lax.rem(slot, room).astype(F32)
        )
        places_ref[...] = filled.astype(F32).astype(BF16)

        local = id_row - (me * vocab).astype(F32)
        wanted = (local >= 0) & (local < vocab)
        wanted = wanted & (rank_row == iota((room, tokens), 0).astype(F32))
        chosen = jnp.sum(jnp.where(wanted, local + 1.0, 0.0), axis=1, keepdims=True) - 1.0
        selector = (chosen == iota((room, vocab), 1).astype(F32)).astype(F32).astype(BF16)
        for piece, copy in enumerate(copies):
            window = slice(piece * cut, (piece + 1) * cut)
            copy.wait()
            part = jnp.dot(selector[:, window], held[window, :], preferred_element_type=F32)
            if piece:
                part = part + found[...]
            if piece < pieces - 1:
                found[...] = part
        rows_ref[...] = part.astype(BF16)

    return call(
        kernel,
        [
            jax.ShapeDtypeStruct((room, plan.features), BF16),
            jax.ShapeDtypeStruct((tokens, slots), BF16),
            jax.ShapeDtypeStruct((8, HD), F32),
        ],
        [ANY_SPEC] * 2,
        [VMEM_SPEC] * 3,
        [
            pltpu.VMEM(gen_ids.shape, jnp.int32),
            pltpu.VMEM(embed_rows.shape, BF16),
            pltpu.VMEM((room, plan.features), F32),
            pltpu.SemaphoreType.DMA,
            pltpu.SemaphoreType.DMA((pieces,)),
        ],
        16,
        in_hbm(gen_ids),
        in_hbm(embed_rows),
    )


def rows_beyond(plan, gen_ids, embed_rows):
    vocab = embed_rows.shape[0]
    ids = gen_ids.reshape(-1)
    owner = ids // vocab
    order = jnp.arange(plan.tokens)
    rank = jnp.sum((owner[:, None] == owner[None]) & (order[None] < order[:, None]), axis=1)
    shifted = jnp.where(rank >= plan.room, ids - lax.axis_index("head") * vocab, -1)
    selector = (shifted[:, None] == jnp.arange(vocab, dtype=jnp.int32)[None]).astype(BF16)

    def kernel(selector_ref, embed_ref, out_ref, held, sem):
        copy = pltpu.make_async_copy(embed_ref, held, sem)
        copy.start()
        copy.wait()
        found = jnp.dot(selector_ref[...], held[...], preferred_element_type=F32)
        out_ref[...] = found.astype(BF16)

    picked = call(
        kernel,
        jax.ShapeDtypeStruct((plan.tokens, plan.features), BF16),
        [VMEM_SPEC, ANY_SPEC],
        VMEM_SPEC,
        [pltpu.VMEM(embed_rows.shape, BF16), pltpu.SemaphoreType.DMA],
        16,
        selector,
        in_hbm(embed_rows),
    )
    step = 1
    while step < plan.head:
        picked = picked + plan.over_head(picked, step)
        step *= 2
    return picked


def bring(after, source):
    def kernel(_, source_ref, out_ref, sems):
        pieces = 4
        size = source.shape[0] // pieces
        copies = [
            pltpu.make_async_copy(
                source_ref.at[pl.ds(k * size, size)], out_ref.at[pl.ds(k * size, size)], sems.at[k]
            )
            for k in range(pieces)
        ]
        for k, copy in enumerate(copies):
            copy.start(priority=k % 2)
        for copy in copies:
            copy.wait()

    return call(
        kernel,
        jax.ShapeDtypeStruct(source.shape, source.dtype),
        [ANY_SPEC] * 2,
        ANY_SPEC,
        [pltpu.SemaphoreType.DMA((4,))],
        4,
        after,
        in_hbm(source),
    )


def prompt_to_swap(plan, after, prompt_keys, prompt_values):
    half = plan.half

    def kernel(_, keys_ref, values_ref, given_keys_ref, given_values_ref, sems):
        window = aligned(1 - lax.rem(lax.axis_index("seq"), CORES), half)
        copies = [
            pltpu.make_async_copy(keys_ref.at[:, window], given_keys_ref, sems.at[0]),
            pltpu.make_async_copy(values_ref.at[:, window], given_values_ref, sems.at[1]),
        ]
        for copy in copies:
            copy.start()
        for copy in copies:
            copy.wait()

    return call(
        kernel,
        [jax.ShapeDtypeStruct((plan.prompt_rows, half), BF16)] * 2,
        [ANY_SPEC] * 3,
        [ANY_SPEC] * 2,
        [pltpu.SemaphoreType.DMA((2,))],
        4,
        after,
        in_hbm(prompt_keys),
        in_hbm(prompt_values),
    )


def gather_embedded(
    plan, gen_ids, embed_rows, w_key, w_value, prompt_keys, prompt_values, w_out
):
    rows, places, beyond = pick(plan, gen_ids, embed_rows)
    rest = lax.cond(
        beyond[0, 0] > 0.5,
        lambda: rows_beyond(plan, gen_ids, embed_rows),
        lambda: jnp.zeros((plan.tokens, plan.features), BF16),
    )
    w_key = bring(rest, w_key)
    across = [plan.over_head(rows, step * plan.inner) for step in range(1, plan.outer)]
    near = jnp.concatenate([rows, *across])
    near, w_key, w_out = lax.optimization_barrier((near, w_key, w_out))
    swapped_out = plan.over_seq(w_out, 1)
    given = prompt_to_swap(plan, near, prompt_keys, prompt_values)
    w_value = bring(near, w_value)
    blocks = [near] + [plan.over_head(near, step) for step in range(1, plan.inner)[::-1]]
    size = plan.outer * plan.room

    def kernel(places_ref, beyond_ref, rest_ref, *refs):
        blocks, (out_ref, held, added, sem) = refs[: plan.inner], refs[plan.inner :]
        for block, ref in enumerate(blocks):
            held[block * size : (block + 1) * size] = ref[...]
        placed = jnp.dot(places_ref[...], held[...], preferred_element_type=F32)
        out_ref[...] = placed.astype(BF16)

        @pl.when(jnp.max(beyond_ref[...]) > 0.5)
        def _():
            copy = pltpu.make_async_copy(rest_ref, added, sem)
            copy.start()
            copy.wait()
            out_ref[...] = out_ref[...] + added[...]

    embedded = call(
        kernel,
        jax.ShapeDtypeStruct((plan.tokens, plan.features), BF16),
        [VMEM_SPEC] * 2 + [ANY_SPEC] + [VMEM_SPEC] * plan.inner,
        VMEM_SPEC,
        [
            pltpu.VMEM((plan.inner * size, plan.features), BF16),
            pltpu.VMEM((plan.tokens, plan.features), BF16),
            pltpu.SemaphoreType.DMA,
        ],
        16,
        places,
        beyond,
        rest,
        *blocks,
    )
    return embedded, w_key, w_value, given, swapped_out


def prompt_half(plan, prompt_keys, prompt_values, after):
    rows, half = plan.prompt_rows, plan.half

    def kernel(_, keys_ref, values_ref, out_ref, sems):
        window = aligned(lax.rem(lax.axis_index("seq"), CORES), half)
        copies = [
            pltpu.make_async_copy(
                source.at[:, window], out_ref.at[pl.ds(place * rows, rows)], sems.at[place]
            )
            for place, source in enumerate((keys_ref, values_ref))
        ]
        for copy in copies:
            copy.start()
        for copy in copies:
            copy.wait()

    return call(
        kernel,
        jax.ShapeDtypeStruct((2 * rows, half), BF16),
        [ANY_SPEC] * 3,
        ANY_SPEC,
        [pltpu.SemaphoreType.DMA((2,))],
        4,
        after,
        in_hbm(prompt_keys),
        in_hbm(prompt_values),
    )


def project_half(plan, embedded, weights, other, dtype):
    half = plan.half

    def kernel(rows_ref, *refs):
        sources, out_ref = refs[:3], refs[3]
        core = lax.rem(lax.axis_index("seq"), CORES)
        window = aligned(1 - core if other else core, half)
        for kind in range(3):
            product = jnp.dot(
                rows_ref[...], sources[kind][:, window], preferred_element_type=F32
            )
            out_ref[:, kind * half : (kind + 1) * half] = product.astype(dtype)

    return call(
        kernel,
        jax.ShapeDtypeStruct((plan.tokens, 3 * half), dtype),
        [VMEM_SPEC] * 4,
        VMEM_SPEC,
        [],
        16,
        embedded,
        *weights,
    )


def sum_cores(plan, own, received):
    tokens, half, owned = plan.tokens, plan.half, plan.owned

    def kernel(own_ref, received_ref, *refs):
        outs, total = refs[: plan.chips], refs[plan.chips]
        total[...] = own_ref[...] + received_ref[...].astype(F32)
        chip = lax.axis_index("seq") // CORES
        for dy in range(plan.chips):
            out, rows = outs[dy], aligned(chip ^ dy, owned)
            out[:tokens] = total[:, :half].astype(out.dtype)
            out[tokens : tokens + owned] = total[rows, half : 2 * half].astype(out.dtype)
            out[tokens + owned :] = total[rows, 2 * half :].astype(out.dtype)

    shape = (tokens + 2 * owned, half)
    return call(
        kernel,
        [jax.ShapeDtypeStruct(shape, BF16 if dy else F32) for dy in range(plan.chips)],
        [VMEM_SPEC] * 2,
        [VMEM_SPEC] * plan.chips,
        [pltpu.VMEM((tokens, 3 * half), F32)],
        8,
        own,
        received,
    )


def project(plan, embedded, weights):
    received = plan.over_seq(project_half(plan, embedded, weights, True, BF16), 1)
    own = project_half(plan, embedded, weights, False, F32)
    parts = sum_cores(plan, own, received)
    return [parts[0]] + [plan.over_seq(parts[dy], dy * CORES) for dy in range(1, plan.chips)]


def angle_tables(plan):
    half_size = HD // 2
    frequency = 10000.0 ** (-jnp.arange(half_size, dtype=F32) / half_size)
    positions = plan.prompt_rows * plan.seq + jnp.arange(plan.steps, dtype=jnp.int32)
    angles = positions.astype(F32)[:, None] * frequency[None, :]
    cosine, sine_part = jnp.cos(angles), jnp.sin(angles)
    return (
        jnp.concatenate([cosine, cosine], axis=-1),
        jnp.concatenate([-sine_part, sine_part], axis=-1),
    )


def attend(plan, parts, kept, swapped, tables):
    tokens, half, owned, share = plan.tokens, plan.half, plan.owned, plan.share
    rows = plan.prompt_rows
    scale = 1.0 / math.sqrt(HD)
    transposed = (((1,), (1,)), ((), ()))

    def kernel(*refs):
        sums, refs = refs[: plan.chips], refs[plan.chips :]
        kept_ref, keys_ref, values_ref, cosine_ref, sine_ref = refs[:5]
        near_ref, far_ref, result = refs[5:]
        core = lax.rem(lax.axis_index("seq"), CORES)
        chip = lax.axis_index("seq") // CORES
        total = sums[0][...]
        for dy in range(1, plan.chips):
            total = total + sums[dy][...].astype(F32)
        cosine, sine_part = cosine_ref[...][None], sine_ref[...][None]

        def rotated(vectors):
            turned = pltpu.roll(vectors, HD // 2, 1)
            shaped = vectors.reshape(-1, plan.steps, HD) * cosine
            shaped = shaped + turned.reshape(-1, plan.steps, HD) * sine_part
            return shaped.reshape(vectors.shape).astype(BF16)

        pair = 2 * HD
        row = lax.broadcasted_iota(jnp.int32, (2 * tokens, 2 * owned), 0)
        column = lax.broadcasted_iota(jnp.int32, (2 * tokens, 2 * owned), 1)
        same_head = row // tokens == column // owned
        row, column = lax.rem(row, tokens), lax.rem(column, owned) + chip * owned
        seen = same_head & (row // plan.steps == column // plan.steps) & (column <= row)
        lane = lax.broadcasted_iota(jnp.int32, (tokens, HD), 1)
        logs = jnp.zeros((tokens, HD), F32)
        nothing = jnp.zeros((tokens, HD), BF16)
        for start in range(0, half, pair):
            lanes = slice(start, start + pair)
            near, far = slice(start, start + HD), slice(start + HD, start + pair)
            query = jnp.concatenate(
                [
                    jnp.concatenate([rotated(total[:tokens, near]), nothing], axis=1),
                    jnp.concatenate([nothing, rotated(total[:tokens, far])], axis=1),
                ]
            )
            keys, values = slice(tokens, tokens + owned), slice(tokens + owned, None)
            gen_key = jnp.concatenate([rotated(total[keys, near]), rotated(total[keys, far])])
            gen_value = jnp.concatenate([total[values, near], total[values, far]]).astype(BF16)

            def score(vectors, key):
                return (
                    lax.dot_general(vectors, key, transposed, preferred_element_type=F32) * scale
                )

            own = score(jnp.concatenate([query[:tokens, :HD], query[tokens:, HD:]]), gen_key)
            scores = [
                score(query, kept_ref[:rows, lanes]),
                score(query, keys_ref[:, lanes]),
                jnp.where(seen, own, -jnp.inf),
            ]
            peak = jnp.max(scores[0], axis=1, keepdims=True)
            for part in scores[1:]:
                peak = jnp.maximum(peak, jnp.max(part, axis=1, keepdims=True))
            weights = [jnp.exp(part - peak) for part in scores]
            weight_sum = sum(jnp.sum(weight, axis=1, keepdims=True) for weight in weights)
            weights = [weight.astype(BF16) for weight in weights]
            summed = jnp.dot(
                weights[0], kept_ref[rows:, lanes], preferred_element_type=F32
            ) + jnp.dot(weights[1], values_ref[:, lanes], preferred_element_type=F32)
            summed = jnp.concatenate([summed[:tokens, :HD], summed[tokens:, HD:]])
            summed = summed + jnp.dot(weights[2], gen_value, preferred_element_type=F32)
            mixed = (summed / weight_sum).astype(BF16)
            result[:, near] = mixed[:tokens]
            result[:, far] = mixed[tokens:]
            both = peak + jnp.log(weight_sum)
            for place, rest in enumerate((both[:tokens], both[tokens:])):
                first = 3 * (start // HD + place)
                for term in range(3):
                    piece = rest.astype(BF16).astype(F32)
                    rest = rest - piece
                    logs = jnp.where(lane == first + term, piece, logs)
        result[:, half:] = logs.astype(BF16)
        for pair in range(plan.chips):
            place = pl.ds(pair * share, share)
            near_ref[place, :] = result[aligned(pair * CORES + core, share), :]
            far_ref[place, :] = result[aligned(pair * CORES + 1 - core, share), :]

    out = jax.ShapeDtypeStruct((tokens // CORES, half + HD), BF16)
    near, far = call(
        kernel,
        [out] * 2,
        [VMEM_SPEC] * (plan.chips + 5),
        [VMEM_SPEC] * 2,
        [pltpu.VMEM((tokens, half + HD), BF16)],
        24,
        *parts,
        kept,
        *swapped,
        *tables,
    )
    got = {k: plan.over_seq(far if k % CORES else near, k) for k in range(1, plan.seq)}
    return [near] + [got[k] for k in range(1, plan.seq)]


def multiply_out(plan, attended, own, swapped):
    share, half, columns = plan.share, plan.half, plan.columns
    rows = plan.tokens // CORES
    keys = [(dy, dx) for dx in range(plan.parts) for dy in range(plan.chips)]

    def kernel(*refs):
        parts, refs = refs[: plan.seq], refs[plan.seq :]
        (own_ref, swapped_ref), refs = refs[:2], refs[2:]
        outs, (joined,) = refs[: len(keys)], refs[len(keys) :]
        seq_index = lax.axis_index("seq")
        chip, core = seq_index // CORES, lax.rem(seq_index, CORES)
        part_index = lax.rem(lax.axis_index("head"), plan.parts)
        for side in range(CORES):
            sources = [parts[step] for step in range(side, plan.seq, CORES)]
            first = (core ^ side) * half
            for head in range(half // HD):
                lanes = slice(head * HD, (head + 1) * HD)
                logs = [
                    sum(
                        source[:, half + 3 * head + term : half + 3 * head + term + 1].astype(F32)
                        for term in (2, 1, 0)
                    )
                    for source in sources
                ]
                top = logs[0]
                for one in logs[1:]:
                    top = jnp.maximum(top, one)
                scales = [jnp.exp(one - top) for one in logs]
                mixed = sum(f * source[:, lanes].astype(F32) for f, source in zip(scales, sources))
                mixed = (mixed / sum(scales)).astype(BF16)
                window = pl.ds(pl.multiple_of(first + head * HD, HD), HD)
                for owner in range(plan.chips):
                    rows_of = mixed[owner * share : (owner + 1) * share]
                    joined[aligned(owner ^ chip, share), window] = rows_of
        left = joined[...]
        for dx in list(range(plan.parts))[::-1]:
            lanes = aligned(part_index ^ dx, columns)
            for weight, block in ((own_ref, core), (swapped_ref, 1 - core)):
                product = jnp.dot(left, weight[:, lanes], preferred_element_type=F32)
                for dy in range(plan.chips):
                    out = outs[keys.index((dy, dx))]
                    out[block] = product[dy * share : (dy + 1) * share].astype(out.dtype)

    shape = (CORES, share, columns)
    outs = [jax.ShapeDtypeStruct(shape, BF16 if any(key) else F32) for key in keys]
    made = call(
        kernel,
        outs,
        [VMEM_SPEC] * (plan.seq + 2),
        [VMEM_SPEC] * len(keys),
        [pltpu.VMEM((rows, plan.width), BF16)],
        24,
        *attended,
        own,
        swapped,
    )
    got = {}
    for key, value in list(zip(keys, made))[::-1]:
        dy, dx = key
        if any(key):
            value = plan.send(value, lambda s, h: (s ^ (dy * CORES), h ^ dx))
        got[key] = value
    return got


def sum_parts(plan, got):
    keys = list(got)
    shape = (plan.share, plan.columns)

    def kernel(*refs):
        ins, refs = dict(zip(keys, refs)), refs[len(keys) :]
        outs, (held,) = refs[: plan.seq], refs[plan.seq :]
        chip = lax.axis_index("seq") // CORES
        place = lax.axis_index("head") // plan.parts
        for dy in range(plan.chips):
            total = ins[dy, 0][...].astype(F32)
            for dx in range(1, plan.parts):
                total = total + ins[dy, dx][...].astype(F32)
            for core in range(CORES):
                held[(chip ^ dy) * CORES + core] = total[core]
        for step in range(plan.seq):
            outs[step][...] = held[place ^ step].astype(outs[step].dtype)

    outs = [jax.ShapeDtypeStruct(shape, BF16 if step else F32) for step in range(plan.seq)]
    made = call(
        kernel,
        outs,
        [VMEM_SPEC] * len(keys),
        [VMEM_SPEC] * plan.seq,
        [pltpu.VMEM((plan.seq,) + shape, F32)],
        16,
        *got.values(),
    )
    got = [
        plan.send(made[step], lambda s, h: (s, h ^ (step * plan.parts)))
        for step in list(range(1, plan.seq))[::-1]
    ]

    def last(*refs):
        total = refs[0][...]
        for ref in refs[1:-1]:
            total = total + ref[...].astype(F32)
        refs[-1][...] = total.astype(BF16)

    return call(
        last,
        jax.ShapeDtypeStruct(shape, BF16),
        [VMEM_SPEC] * plan.seq,
        VMEM_SPEC,
        [],
        8,
        made[0],
        *got,
    )


def solution(mesh):
    def body(gen_ids, embed_rows, w_query, w_key, w_value, w_out, prompt_keys, prompt_values):
        plan = Plan(mesh, gen_ids, w_query, w_out, prompt_keys)
        embedded, w_key, w_value, given, swapped_out = gather_embedded(
            plan, gen_ids, embed_rows, w_key, w_value, prompt_keys, prompt_values, w_out
        )
        swapped = [plan.over_seq(part, 1) for part in given]
        parts = project(plan, embedded, (w_query, w_key, w_value))
        kept = prompt_half(plan, prompt_keys, prompt_values, parts[0])
        attended = attend(plan, parts, kept, swapped, angle_tables(plan))
        return sum_parts(plan, multiply_out(plan, attended, w_out, swapped_out))

    return jax.shard_map(
        body,
        mesh=mesh,
        in_specs=(
            P(),
            P("head", "seq"),
            P("seq", "head"),
            P("seq", "head"),
            P("seq", "head"),
            P("head", "seq"),
            P("seq", "head"),
            P("seq", "head"),
        ),
        out_specs=P("seq", "head"),
        check_vma=False,
    )
```

```python
import math

import jax
import jax.numpy as jnp
from jax import lax
from jax.experimental import pallas as pl
from jax.experimental.pallas import tpu as pltpu
from jax.sharding import PartitionSpec as P

HD = 128
CORES = 2
MIB = 1 << 20
BF16 = jnp.bfloat16
F32 = jnp.float32


class Plan:
    def __init__(self, mesh, gen_ids, w_query, w_out, prompt_keys):
        self.seq, self.head = mesh.shape["seq"], mesh.shape["head"]
        self.cands, self.steps = gen_ids.shape
        self.tokens = self.cands * self.steps
        self.features, self.width = w_query.shape
        self.prompt_rows = prompt_keys.shape[0]
        self.inner = math.gcd(self.head, 4)
        self.outer = self.head // self.inner
        self.room = -(-2 * self.tokens // (self.head * 16)) * 16
        self.half = self.width // CORES
        self.chips = self.seq // CORES
        self.parts = self.head // self.seq
        self.share = self.tokens // self.seq
        self.owned = self.tokens // self.chips
        self.columns = w_out.shape[1] // self.parts

    def send(self, value, route):
        pairs = []
        for s in range(self.seq):
            for h in range(self.head):
                to_s, to_h = route(s, h)
                pairs.append((s * self.head + h, to_s * self.head + to_h))
        return lax.ppermute(value, ("seq", "head"), pairs)

    def over_seq(self, value, step):
        return self.send(value, lambda s, h: (s ^ step, h))

    def over_head(self, value, step):
        return self.send(value, lambda s, h: (s, h ^ step))


VMEM_SPEC = pl.BlockSpec(memory_space=pltpu.VMEM)
ANY_SPEC = pl.BlockSpec(memory_space=pl.ANY)


def aligned(index, size):
    return pl.ds(pl.multiple_of(index * size, size), size)


def in_hbm(value):
    return pltpu.with_memory_space_constraint(value, pltpu.HBM)


def call(kernel, out_shape, in_specs, out_specs, scratch, limit, *args, cost=None):
    return pl.pallas_call(
        kernel,
        out_shape=out_shape,
        in_specs=in_specs,
        out_specs=out_specs,
        scratch_shapes=scratch,
        cost_estimate=cost,
        compiler_params=pltpu.CompilerParams(vmem_limit_bytes=limit * MIB),
    )(*args)


def pick(plan, gen_ids, embed_rows):
    vocab = embed_rows.shape[0]
    tokens, steps, room = plan.tokens, plan.steps, plan.room
    cut = 2 * HD
    pieces = vocab // cut
    slots = plan.head * room

    def iota(shape, axis):
        return lax.broadcasted_iota(jnp.int32, shape, axis)

    def kernel(ids_ref, embed_ref, rows_ref, places_ref, beyond_ref, *scratch):
        ids, held, found, ids_sem, sems = scratch
        ids_copy = pltpu.make_async_copy(ids_ref, ids, ids_sem)
        ids_copy.start()
        copies = []
        for piece in range(pieces):
            window = pl.ds(piece * cut, cut)
            copies.append(
                pltpu.make_async_copy(embed_ref.at[window], held.at[window], sems.at[piece])
            )
            copies[-1].start(priority=piece % 2)
        me = lax.axis_index("head")
        ids_copy.wait()
        corner = iota((steps, steps), 0) == iota((steps, steps), 1)
        columns = []
        for cand in range(plan.cands):
            row = ids[cand : cand + 1, :].astype(F32)
            columns.append(jnp.sum(jnp.where(corner, row, 0.0), axis=1, keepdims=True))
        id_column = jnp.concatenate(columns)
        owner_column = id_column.astype(jnp.int32) // vocab

        member = (owner_column == iota((tokens, HD), 1)).astype(F32).astype(BF16)
        same = lax.dot_general(
            member, member, (((1,), (1,)), ((), ())), preferred_element_type=F32
        )
        first, second = iota((tokens, tokens), 0), iota((tokens, tokens), 1)
        rank_column = jnp.sum(jnp.where(second < first, same, 0.0), axis=1, keepdims=True)
        rank_row = jnp.sum(jnp.where(first < second, same, 0.0), axis=0, keepdims=True)
        id_row = jnp.sum(jnp.where(first == second, id_column, 0.0), axis=0, keepdims=True)
        beyond = jnp.sum(jnp.where(rank_column >= room, 1.0, 0.0), axis=0, keepdims=True)
        beyond_ref[...] = jnp.broadcast_to(beyond, beyond_ref.shape)

        slot = iota((tokens, slots), 1)
        place = slot // (plan.outer * room)
        group = lax.rem(slot // room, plan.outer)
        distance = lax.rem(plan.inner - place, plan.inner) + group * plan.inner
        filled = (owner_column == (me ^ distance)) & (
            rank_column == lax.rem(slot, room).astype(F32)
        )
        places_ref[...] = filled.astype(F32).astype(BF16)

        local = id_row - (me * vocab).astype(F32)
        wanted = (local >= 0) & (local < vocab)
        wanted = wanted & (rank_row == iota((room, tokens), 0).astype(F32))
        chosen = jnp.sum(jnp.where(wanted, local + 1.0, 0.0), axis=1, keepdims=True) - 1.0
        selector = (chosen == iota((room, vocab), 1).astype(F32)).astype(F32).astype(BF16)
        for piece, copy in enumerate(copies):
            window = slice(piece * cut, (piece + 1) * cut)
            copy.wait()
            part = jnp.dot(selector[:, window], held[window, :], preferred_element_type=F32)
            if piece:
                part = part + found[...]
            if piece < pieces - 1:
                found[...] = part
        rows_ref[...] = part.astype(BF16)

    return call(
        kernel,
        [
            jax.ShapeDtypeStruct((room, plan.features), BF16),
            jax.ShapeDtypeStruct((tokens, slots), BF16),
            jax.ShapeDtypeStruct((8, HD), F32),
        ],
        [ANY_SPEC] * 2,
        [VMEM_SPEC] * 3,
        [
            pltpu.VMEM(gen_ids.shape, jnp.int32),
            pltpu.VMEM(embed_rows.shape, BF16),
            pltpu.VMEM((room, plan.features), F32),
            pltpu.SemaphoreType.DMA,
            pltpu.SemaphoreType.DMA((pieces,)),
        ],
        16,
        in_hbm(gen_ids),
        in_hbm(embed_rows),
    )


def rows_beyond(plan, gen_ids, embed_rows):
    vocab = embed_rows.shape[0]
    ids = gen_ids.reshape(-1)
    owner = ids // vocab
    order = jnp.arange(plan.tokens)
    rank = jnp.sum((owner[:, None] == owner[None]) & (order[None] < order[:, None]), axis=1)
    shifted = jnp.where(rank >= plan.room, ids - lax.axis_index("head") * vocab, -1)
    selector = (shifted[:, None] == jnp.arange(vocab, dtype=jnp.int32)[None]).astype(BF16)

    def kernel(selector_ref, embed_ref, out_ref, held, sem):
        copy = pltpu.make_async_copy(embed_ref, held, sem)
        copy.start()
        copy.wait()
        found = jnp.dot(selector_ref[...], held[...], preferred_element_type=F32)
        out_ref[...] = found.astype(BF16)

    picked = call(
        kernel,
        jax.ShapeDtypeStruct((plan.tokens, plan.features), BF16),
        [VMEM_SPEC, ANY_SPEC],
        VMEM_SPEC,
        [pltpu.VMEM(embed_rows.shape, BF16), pltpu.SemaphoreType.DMA],
        16,
        selector,
        in_hbm(embed_rows),
    )
    step = 1
    while step < plan.head:
        picked = picked + plan.over_head(picked, step)
        step *= 2
    return picked


def bring(after, source):
    def kernel(_, source_ref, out_ref, sems):
        pieces = 4
        size = source.shape[0] // pieces
        copies = [
            pltpu.make_async_copy(
                source_ref.at[pl.ds(k * size, size)], out_ref.at[pl.ds(k * size, size)], sems.at[k]
            )
            for k in range(pieces)
        ]
        for k, copy in enumerate(copies):
            copy.start(priority=k % 2)
        for copy in copies:
            copy.wait()

    return call(
        kernel,
        jax.ShapeDtypeStruct(source.shape, source.dtype),
        [ANY_SPEC] * 2,
        ANY_SPEC,
        [pltpu.SemaphoreType.DMA((4,))],
        4,
        after,
        in_hbm(source),
    )


def prompt_to_swap(plan, after, prompt_keys, prompt_values):
    half = plan.half

    def kernel(_, keys_ref, values_ref, given_keys_ref, given_values_ref, sems):
        window = aligned(1 - lax.rem(lax.axis_index("seq"), CORES), half)
        copies = [
            pltpu.make_async_copy(keys_ref.at[:, window], given_keys_ref, sems.at[0]),
            pltpu.make_async_copy(values_ref.at[:, window], given_values_ref, sems.at[1]),
        ]
        for copy in copies:
            copy.start()
        for copy in copies:
            copy.wait()

    return call(
        kernel,
        [jax.ShapeDtypeStruct((plan.prompt_rows, half), BF16)] * 2,
        [ANY_SPEC] * 3,
        [ANY_SPEC] * 2,
        [pltpu.SemaphoreType.DMA((2,))],
        4,
        after,
        in_hbm(prompt_keys),
        in_hbm(prompt_values),
    )


def gather_embedded(
    plan, gen_ids, embed_rows, w_key, w_value, prompt_keys, prompt_values, swapped_out
):
    rows, places, beyond = pick(plan, gen_ids, embed_rows)
    rest = lax.cond(
        beyond[0, 0] > 0.5,
        lambda: rows_beyond(plan, gen_ids, embed_rows),
        lambda: jnp.zeros((plan.tokens, plan.features), BF16),
    )
    w_key = bring(rest, w_key)
    across = [plan.over_head(rows, step * plan.inner) for step in range(1, plan.outer)]
    near = jnp.concatenate([rows, *across])
    near, w_key, swapped_out = lax.optimization_barrier((near, w_key, swapped_out))
    given = prompt_to_swap(plan, near, prompt_keys, prompt_values)
    w_value = bring(near, w_value)
    blocks = [near] + [plan.over_head(near, step) for step in range(1, plan.inner)[::-1]]
    size = plan.outer * plan.room

    def kernel(places_ref, beyond_ref, rest_ref, *refs):
        blocks, (out_ref, held, added, sem) = refs[: plan.inner], refs[plan.inner :]
        for block, ref in enumerate(blocks):
            held[block * size : (block + 1) * size] = ref[...]
        placed = jnp.dot(places_ref[...], held[...], preferred_element_type=F32)
        out_ref[...] = placed.astype(BF16)

        @pl.when(jnp.max(beyond_ref[...]) > 0.5)
        def _():
            copy = pltpu.make_async_copy(rest_ref, added, sem)
            copy.start()
            copy.wait()
            out_ref[...] = out_ref[...] + added[...]

    embedded = call(
        kernel,
        jax.ShapeDtypeStruct((plan.tokens, plan.features), BF16),
        [VMEM_SPEC] * 2 + [ANY_SPEC] + [VMEM_SPEC] * plan.inner,
        VMEM_SPEC,
        [
            pltpu.VMEM((plan.inner * size, plan.features), BF16),
            pltpu.VMEM((plan.tokens, plan.features), BF16),
            pltpu.SemaphoreType.DMA,
        ],
        16,
        places,
        beyond,
        rest,
        *blocks,
    )
    return embedded, w_key, w_value, given, swapped_out


def prompt_half(plan, prompt_keys, prompt_values, after):
    rows, half = plan.prompt_rows, plan.half

    def kernel(_, keys_ref, values_ref, out_ref, sems):
        window = aligned(lax.rem(lax.axis_index("seq"), CORES), half)
        copies = [
            pltpu.make_async_copy(
                source.at[:, window], out_ref.at[pl.ds(place * rows, rows)], sems.at[place]
            )
            for place, source in enumerate((keys_ref, values_ref))
        ]
        for copy in copies:
            copy.start()
        for copy in copies:
            copy.wait()

    return call(
        kernel,
        jax.ShapeDtypeStruct((2 * rows, half), BF16),
        [ANY_SPEC] * 3,
        ANY_SPEC,
        [pltpu.SemaphoreType.DMA((2,))],
        4,
        after,
        in_hbm(prompt_keys),
        in_hbm(prompt_values),
    )


def project_half(plan, embedded, weights, other, dtype):
    half = plan.half

    def kernel(rows_ref, *refs):
        sources, out_ref = refs[:3], refs[3]
        core = lax.rem(lax.axis_index("seq"), CORES)
        window = aligned(1 - core if other else core, half)
        for kind in range(3):
            product = jnp.dot(
                rows_ref[...], sources[kind][:, window], preferred_element_type=F32
            )
            out_ref[:, kind * half : (kind + 1) * half] = product.astype(dtype)

    return call(
        kernel,
        jax.ShapeDtypeStruct((plan.tokens, 3 * half), dtype),
        [VMEM_SPEC] * 4,
        VMEM_SPEC,
        [],
        16,
        embedded,
        *weights,
    )


def sum_cores(plan, own, received):
    tokens, half, owned = plan.tokens, plan.half, plan.owned

    def kernel(own_ref, received_ref, *refs):
        outs, total = refs[: plan.chips], refs[plan.chips]
        total[...] = own_ref[...] + received_ref[...].astype(F32)
        chip = lax.axis_index("seq") // CORES
        for dy in range(plan.chips):
            out, rows = outs[dy], aligned(chip ^ dy, owned)
            out[:tokens] = total[:, :half].astype(out.dtype)
            out[tokens : tokens + owned] = total[rows, half : 2 * half].astype(out.dtype)
            out[tokens + owned :] = total[rows, 2 * half :].astype(out.dtype)

    shape = (tokens + 2 * owned, half)
    return call(
        kernel,
        [jax.ShapeDtypeStruct(shape, BF16 if dy else F32) for dy in range(plan.chips)],
        [VMEM_SPEC] * 2,
        [VMEM_SPEC] * plan.chips,
        [pltpu.VMEM((tokens, 3 * half), F32)],
        8,
        own,
        received,
    )


def project(plan, embedded, weights):
    received = plan.over_seq(project_half(plan, embedded, weights, True, BF16), 1)
    own = project_half(plan, embedded, weights, False, F32)
    parts = sum_cores(plan, own, received)
    return [parts[0]] + [plan.over_seq(parts[dy], dy * CORES) for dy in range(1, plan.chips)]


def angle_tables(plan):
    half_size = HD // 2
    frequency = 10000.0 ** (-jnp.arange(half_size, dtype=F32) / half_size)
    positions = plan.prompt_rows * plan.seq + jnp.arange(plan.steps, dtype=jnp.int32)
    angles = positions.astype(F32)[:, None] * frequency[None, :]
    cosine, sine_part = jnp.cos(angles), jnp.sin(angles)
    return (
        jnp.concatenate([cosine, cosine], axis=-1),
        jnp.concatenate([-sine_part, sine_part], axis=-1),
    )


def attend(plan, parts, kept, swapped, tables):
    tokens, half, owned, share = plan.tokens, plan.half, plan.owned, plan.share
    rows = plan.prompt_rows
    scale = 1.0 / math.sqrt(HD)
    transposed = (((1,), (1,)), ((), ()))

    def kernel(*refs):
        sums, refs = refs[: plan.chips], refs[plan.chips :]
        kept_ref, keys_ref, values_ref, cosine_ref, sine_ref = refs[:5]
        near_ref, far_ref, result = refs[5:]
        core = lax.rem(lax.axis_index("seq"), CORES)
        chip = lax.axis_index("seq") // CORES
        total = sums[0][...]
        for dy in range(1, plan.chips):
            total = total + sums[dy][...].astype(F32)
        cosine, sine_part = cosine_ref[...][None], sine_ref[...][None]

        def rotated(vectors):
            turned = pltpu.roll(vectors, HD // 2, 1)
            shaped = vectors.reshape(-1, plan.steps, HD) * cosine
            shaped = shaped + turned.reshape(-1, plan.steps, HD) * sine_part
            return shaped.reshape(vectors.shape).astype(BF16)

        pair = 2 * HD
        row = lax.broadcasted_iota(jnp.int32, (2 * tokens, 2 * owned), 0)
        column = lax.broadcasted_iota(jnp.int32, (2 * tokens, 2 * owned), 1)
        same_head = row // tokens == column // owned
        row, column = lax.rem(row, tokens), lax.rem(column, owned) + chip * owned
        seen = same_head & (row // plan.steps == column // plan.steps) & (column <= row)
        lane = lax.broadcasted_iota(jnp.int32, (tokens, HD), 1)
        logs = jnp.zeros((tokens, HD), F32)
        nothing = jnp.zeros((tokens, HD), BF16)
        for start in range(0, half, pair):
            lanes = slice(start, start + pair)
            near, far = slice(start, start + HD), slice(start + HD, start + pair)
            query = jnp.concatenate(
                [
                    jnp.concatenate([rotated(total[:tokens, near]), nothing], axis=1),
                    jnp.concatenate([nothing, rotated(total[:tokens, far])], axis=1),
                ]
            )
            keys, values = slice(tokens, tokens + owned), slice(tokens + owned, None)
            gen_key = jnp.concatenate([rotated(total[keys, near]), rotated(total[keys, far])])
            gen_value = jnp.concatenate([total[values, near], total[values, far]]).astype(BF16)

            def score(vectors, key):
                return (
                    lax.dot_general(vectors, key, transposed, preferred_element_type=F32) * scale
                )

            own = score(jnp.concatenate([query[:tokens, :HD], query[tokens:, HD:]]), gen_key)
            scores = [
                score(query, kept_ref[:rows, lanes]),
                score(query, keys_ref[:, lanes]),
                jnp.where(seen, own, -jnp.inf),
            ]
            peak = jnp.max(scores[0], axis=1, keepdims=True)
            for part in scores[1:]:
                peak = jnp.maximum(peak, jnp.max(part, axis=1, keepdims=True))
            weights = [jnp.exp(part - peak) for part in scores]
            weight_sum = sum(jnp.sum(weight, axis=1, keepdims=True) for weight in weights)
            weights = [weight.astype(BF16) for weight in weights]
            summed = jnp.dot(
                weights[0], kept_ref[rows:, lanes], preferred_element_type=F32
            ) + jnp.dot(weights[1], values_ref[:, lanes], preferred_element_type=F32)
            summed = jnp.concatenate([summed[:tokens, :HD], summed[tokens:, HD:]])
            summed = summed + jnp.dot(weights[2], gen_value, preferred_element_type=F32)
            mixed = (summed / weight_sum).astype(BF16)
            result[:, near] = mixed[:tokens]
            result[:, far] = mixed[tokens:]
            both = peak + jnp.log(weight_sum)
            for place, rest in enumerate((both[:tokens], both[tokens:])):
                first = 3 * (start // HD + place)
                for term in range(3):
                    piece = rest.astype(BF16).astype(F32)
                    rest = rest - piece
                    logs = jnp.where(lane == first + term, piece, logs)
        result[:, half:] = logs.astype(BF16)
        for pair in range(plan.chips):
            place = pl.ds(pair * share, share)
            near_ref[place, :] = result[aligned(pair * CORES + core, share), :]
            far_ref[place, :] = result[aligned(pair * CORES + 1 - core, share), :]

    out = jax.ShapeDtypeStruct((tokens // CORES, half + HD), BF16)
    near, far = call(
        kernel,
        [out] * 2,
        [VMEM_SPEC] * (plan.chips + 5),
        [VMEM_SPEC] * 2,
        [pltpu.VMEM((tokens, half + HD), BF16)],
        24,
        *parts,
        kept,
        *swapped,
        *tables,
    )
    got = {k: plan.over_seq(far if k % CORES else near, k) for k in range(1, plan.seq)}
    return [near] + [got[k] for k in range(1, plan.seq)]


def multiply_out(plan, attended, own, swapped):
    share, half, columns = plan.share, plan.half, plan.columns
    rows = plan.tokens // CORES
    keys = [(dy, dx) for dx in range(plan.parts) for dy in range(plan.chips)]

    def kernel(*refs):
        parts, refs = refs[: plan.seq], refs[plan.seq :]
        (own_ref, swapped_ref), refs = refs[:2], refs[2:]
        outs, (joined,) = refs[: len(keys)], refs[len(keys) :]
        seq_index = lax.axis_index("seq")
        chip, core = seq_index // CORES, lax.rem(seq_index, CORES)
        part_index = lax.rem(lax.axis_index("head"), plan.parts)
        for side in range(CORES):
            sources = [parts[step] for step in range(side, plan.seq, CORES)]
            first = (core ^ side) * half
            for head in range(half // HD):
                lanes = slice(head * HD, (head + 1) * HD)
                logs = [
                    sum(
                        source[:, half + 3 * head + term : half + 3 * head + term + 1].astype(F32)
                        for term in (2, 1, 0)
                    )
                    for source in sources
                ]
                top = logs[0]
                for one in logs[1:]:
                    top = jnp.maximum(top, one)
                scales = [jnp.exp(one - top) for one in logs]
                mixed = sum(f * source[:, lanes].astype(F32) for f, source in zip(scales, sources))
                mixed = (mixed / sum(scales)).astype(BF16)
                window = pl.ds(pl.multiple_of(first + head * HD, HD), HD)
                for owner in range(plan.chips):
                    rows_of = mixed[owner * share : (owner + 1) * share]
                    joined[aligned(owner ^ chip, share), window] = rows_of
        left = joined[...]
        for dx in list(range(plan.parts))[::-1]:
            lanes = aligned(part_index ^ dx, columns)
            for weight, block in ((own_ref, core), (swapped_ref, 1 - core)):
                product = jnp.dot(left, weight[:, lanes], preferred_element_type=F32)
                for dy in range(plan.chips):
                    out = outs[keys.index((dy, dx))]
                    out[block] = product[dy * share : (dy + 1) * share].astype(out.dtype)

    shape = (CORES, share, columns)
    outs = [jax.ShapeDtypeStruct(shape, BF16 if any(key) else F32) for key in keys]
    made = call(
        kernel,
        outs,
        [VMEM_SPEC] * (plan.seq + 2),
        [VMEM_SPEC] * len(keys),
        [pltpu.VMEM((rows, plan.width), BF16)],
        24,
        *attended,
        own,
        swapped,
    )
    got = {}
    for key, value in list(zip(keys, made))[::-1]:
        dy, dx = key
        if any(key):
            value = plan.send(value, lambda s, h: (s ^ (dy * CORES), h ^ dx))
        got[key] = value
    return got


def sum_parts(plan, got):
    keys = list(got)
    shape = (plan.share, plan.columns)

    def kernel(*refs):
        ins, refs = dict(zip(keys, refs)), refs[len(keys) :]
        outs, (held,) = refs[: plan.seq], refs[plan.seq :]
        chip = lax.axis_index("seq") // CORES
        place = lax.axis_index("head") // plan.parts
        for dy in range(plan.chips):
            total = ins[dy, 0][...].astype(F32)
            for dx in range(1, plan.parts):
                total = total + ins[dy, dx][...].astype(F32)
            for core in range(CORES):
                held[(chip ^ dy) * CORES + core] = total[core]
        for step in range(plan.seq):
            outs[step][...] = held[place ^ step].astype(outs[step].dtype)

    outs = [jax.ShapeDtypeStruct(shape, BF16 if step else F32) for step in range(plan.seq)]
    made = call(
        kernel,
        outs,
        [VMEM_SPEC] * len(keys),
        [VMEM_SPEC] * plan.seq,
        [pltpu.VMEM((plan.seq,) + shape, F32)],
        16,
        *got.values(),
    )
    got = [
        plan.send(made[step], lambda s, h: (s, h ^ (step * plan.parts)))
        for step in list(range(1, plan.seq))[::-1]
    ]

    def last(*refs):
        total = refs[0][...]
        for ref in refs[1:-1]:
            total = total + ref[...].astype(F32)
        refs[-1][...] = total.astype(BF16)

    return call(
        last,
        jax.ShapeDtypeStruct(shape, BF16),
        [VMEM_SPEC] * plan.seq,
        VMEM_SPEC,
        [],
        8,
        made[0],
        *got,
    )


def solution(mesh):
    def body(gen_ids, embed_rows, w_query, w_key, w_value, w_out, prompt_keys, prompt_values):
        plan = Plan(mesh, gen_ids, w_query, w_out, prompt_keys)
        swapped_out = plan.over_seq(w_out, 1)
        embedded, w_key, w_value, given, swapped_out = gather_embedded(
            plan, gen_ids, embed_rows, w_key, w_value, prompt_keys, prompt_values, swapped_out
        )
        swapped = [plan.over_seq(part, 1) for part in given]
        parts = project(plan, embedded, (w_query, w_key, w_value))
        kept = prompt_half(plan, prompt_keys, prompt_values, parts[0])
        swapped_out = bring(parts[0], swapped_out)
        attended = attend(plan, parts, kept, swapped, angle_tables(plan))
        return sum_parts(plan, multiply_out(plan, attended, w_out, swapped_out))

    return jax.shard_map(
        body,
        mesh=mesh,
        in_specs=(
            P(),
            P("head", "seq"),
            P("seq", "head"),
            P("seq", "head"),
            P("seq", "head"),
            P("head", "seq"),
            P("seq", "head"),
            P("seq", "head"),
        ),
        out_specs=P("seq", "head"),
        check_vma=False,
    )
```

```python
import math

import jax
import jax.numpy as jnp
from jax import lax
from jax.experimental import pallas as pl
from jax.experimental.pallas import tpu as pltpu
from jax.sharding import PartitionSpec as P

HD = 128
CORES = 2
MIB = 1 << 20
BF16 = jnp.bfloat16
F32 = jnp.float32


class Plan:
    def __init__(self, mesh, gen_ids, w_query, w_out, prompt_keys):
        self.seq, self.head = mesh.shape["seq"], mesh.shape["head"]
        self.cands, self.steps = gen_ids.shape
        self.tokens = self.cands * self.steps
        self.features, self.width = w_query.shape
        self.prompt_rows = prompt_keys.shape[0]
        self.inner = math.gcd(self.head, 4)
        self.outer = self.head // self.inner
        self.room = -(-2 * self.tokens // (self.head * 16)) * 16
        self.half = self.width // CORES
        self.chips = self.seq // CORES
        self.parts = self.head // self.seq
        self.share = self.tokens // self.seq
        self.owned = self.tokens // self.chips
        self.columns = w_out.shape[1] // self.parts

    def send(self, value, route):
        pairs = []
        for s in range(self.seq):
            for h in range(self.head):
                to_s, to_h = route(s, h)
                pairs.append((s * self.head + h, to_s * self.head + to_h))
        return lax.ppermute(value, ("seq", "head"), pairs)

    def over_seq(self, value, step):
        return self.send(value, lambda s, h: (s ^ step, h))

    def over_head(self, value, step):
        return self.send(value, lambda s, h: (s, h ^ step))


VMEM_SPEC = pl.BlockSpec(memory_space=pltpu.VMEM)
ANY_SPEC = pl.BlockSpec(memory_space=pl.ANY)


def aligned(index, size):
    return pl.ds(pl.multiple_of(index * size, size), size)


def in_hbm(value):
    return pltpu.with_memory_space_constraint(value, pltpu.HBM)


def call(kernel, out_shape, in_specs, out_specs, scratch, limit, *args, cost=None):
    return pl.pallas_call(
        kernel,
        out_shape=out_shape,
        in_specs=in_specs,
        out_specs=out_specs,
        scratch_shapes=scratch,
        cost_estimate=cost,
        compiler_params=pltpu.CompilerParams(vmem_limit_bytes=limit * MIB),
    )(*args)


def iota(shape, axis):
    return lax.broadcasted_iota(jnp.int32, shape, axis)


def id_columns(plan, ids):
    steps = plan.steps
    corner = iota((steps, steps), 0) == iota((steps, steps), 1)
    columns = []
    for cand in range(plan.cands):
        row = ids[cand : cand + 1, :].astype(F32)
        columns.append(jnp.sum(jnp.where(corner, row, 0.0), axis=1, keepdims=True))
    return jnp.concatenate(columns)


def pick(plan, gen_ids, embed_rows):
    vocab = embed_rows.shape[0]
    tokens, room = plan.tokens, plan.room
    cut = 2 * HD
    pieces = vocab // cut

    def kernel(ids_ref, embed_ref, rows_ref, ids, held, found, ids_sem, sems):
        ids_copy = pltpu.make_async_copy(ids_ref, ids, ids_sem)
        ids_copy.start()
        copies = []
        for piece in range(pieces):
            window = pl.ds(piece * cut, cut)
            copies.append(
                pltpu.make_async_copy(embed_ref.at[window], held.at[window], sems.at[piece])
            )
            copies[-1].start(priority=piece % 2)
        base = (lax.axis_index("head") * vocab).astype(F32)
        first, second = iota((tokens, tokens), 0), iota((tokens, tokens), 1)
        ids_copy.wait()
        column = id_columns(plan, ids) - base
        local = (column >= 0) & (column < vocab)
        row = jnp.sum(jnp.where(first == second, column, 0.0), axis=0, keepdims=True)
        earlier = jnp.where((first < second) & local, 1.0, 0.0)
        rank = jnp.sum(earlier, axis=0, keepdims=True)
        wanted = (row >= 0) & (row < vocab) & (rank == iota((room, tokens), 0).astype(F32))
        chosen = jnp.sum(jnp.where(wanted, row + 1.0, 0.0), axis=1, keepdims=True) - 1.0
        selector = (chosen == iota((room, vocab), 1).astype(F32)).astype(F32).astype(BF16)
        for piece, copy in enumerate(copies):
            window = slice(piece * cut, (piece + 1) * cut)
            copy.wait()
            part = jnp.dot(selector[:, window], held[window, :], preferred_element_type=F32)
            if piece:
                part = part + found[...]
            if piece < pieces - 1:
                found[...] = part
        rows_ref[...] = part.astype(BF16)

    return call(
        kernel,
        jax.ShapeDtypeStruct((room, plan.features), BF16),
        [ANY_SPEC] * 2,
        VMEM_SPEC,
        [
            pltpu.VMEM(gen_ids.shape, jnp.int32),
            pltpu.VMEM(embed_rows.shape, BF16),
            pltpu.VMEM((room, plan.features), F32),
            pltpu.SemaphoreType.DMA,
            pltpu.SemaphoreType.DMA((pieces,)),
        ],
        16,
        in_hbm(gen_ids),
        in_hbm(embed_rows),
    )


def find_places(plan, after, gen_ids, vocab):
    tokens, room = plan.tokens, plan.room
    slots = plan.head * room

    def kernel(_, ids_ref, places_ref, beyond_ref, ids, ids_sem):
        ids_copy = pltpu.make_async_copy(ids_ref, ids, ids_sem)
        ids_copy.start()
        ids_copy.wait()
        owner = id_columns(plan, ids).astype(jnp.int32) // vocab
        member = (owner == iota((tokens, HD), 1)).astype(F32).astype(BF16)
        same = lax.dot_general(
            member, member, (((1,), (1,)), ((), ())), preferred_element_type=F32
        )
        earlier = iota((tokens, tokens), 1) < iota((tokens, tokens), 0)
        rank = jnp.sum(jnp.where(earlier, same, 0.0), axis=1, keepdims=True)
        beyond = jnp.sum(jnp.where(rank >= room, 1.0, 0.0), axis=0, keepdims=True)
        beyond_ref[...] = jnp.broadcast_to(beyond, beyond_ref.shape)
        slot = iota((tokens, slots), 1)
        place = slot // (plan.outer * room)
        group = lax.rem(slot // room, plan.outer)
        distance = lax.rem(plan.inner - place, plan.inner) + group * plan.inner
        filled = (owner == (lax.axis_index("head") ^ distance)) & (
            rank == lax.rem(slot, room).astype(F32)
        )
        places_ref[...] = filled.astype(F32).astype(BF16)

    return call(
        kernel,
        [
            jax.ShapeDtypeStruct((tokens, slots), BF16),
            jax.ShapeDtypeStruct((8, HD), F32),
        ],
        [ANY_SPEC] * 2,
        [VMEM_SPEC] * 2,
        [pltpu.VMEM(gen_ids.shape, jnp.int32), pltpu.SemaphoreType.DMA],
        8,
        after,
        in_hbm(gen_ids),
    )


def rows_beyond(plan, gen_ids, embed_rows):
    vocab = embed_rows.shape[0]
    ids = gen_ids.reshape(-1)
    owner = ids // vocab
    order = jnp.arange(plan.tokens)
    rank = jnp.sum((owner[:, None] == owner[None]) & (order[None] < order[:, None]), axis=1)
    shifted = jnp.where(rank >= plan.room, ids - lax.axis_index("head") * vocab, -1)
    selector = (shifted[:, None] == jnp.arange(vocab, dtype=jnp.int32)[None]).astype(BF16)

    def kernel(selector_ref, embed_ref, out_ref, held, sem):
        copy = pltpu.make_async_copy(embed_ref, held, sem)
        copy.start()
        copy.wait()
        found = jnp.dot(selector_ref[...], held[...], preferred_element_type=F32)
        out_ref[...] = found.astype(BF16)

    picked = call(
        kernel,
        jax.ShapeDtypeStruct((plan.tokens, plan.features), BF16),
        [VMEM_SPEC, ANY_SPEC],
        VMEM_SPEC,
        [pltpu.VMEM(embed_rows.shape, BF16), pltpu.SemaphoreType.DMA],
        16,
        selector,
        in_hbm(embed_rows),
    )
    step = 1
    while step < plan.head:
        picked = picked + plan.over_head(picked, step)
        step *= 2
    return picked


def bring(after, source):
    def kernel(_, source_ref, out_ref, sems):
        pieces = 4
        size = source.shape[0] // pieces
        copies = [
            pltpu.make_async_copy(
                source_ref.at[pl.ds(k * size, size)], out_ref.at[pl.ds(k * size, size)], sems.at[k]
            )
            for k in range(pieces)
        ]
        for k, copy in enumerate(copies):
            copy.start(priority=k % 2)
        for copy in copies:
            copy.wait()

    return call(
        kernel,
        jax.ShapeDtypeStruct(source.shape, source.dtype),
        [ANY_SPEC] * 2,
        ANY_SPEC,
        [pltpu.SemaphoreType.DMA((4,))],
        4,
        after,
        in_hbm(source),
    )


def prompt_to_swap(plan, after, prompt_keys, prompt_values):
    half = plan.half

    def kernel(_, keys_ref, values_ref, given_keys_ref, given_values_ref, sems):
        window = aligned(1 - lax.rem(lax.axis_index("seq"), CORES), half)
        copies = [
            pltpu.make_async_copy(keys_ref.at[:, window], given_keys_ref, sems.at[0]),
            pltpu.make_async_copy(values_ref.at[:, window], given_values_ref, sems.at[1]),
        ]
        for copy in copies:
            copy.start()
        for copy in copies:
            copy.wait()

    return call(
        kernel,
        [jax.ShapeDtypeStruct((plan.prompt_rows, half), BF16)] * 2,
        [ANY_SPEC] * 3,
        [ANY_SPEC] * 2,
        [pltpu.SemaphoreType.DMA((2,))],
        4,
        after,
        in_hbm(prompt_keys),
        in_hbm(prompt_values),
    )


def gather_embedded(
    plan, gen_ids, embed_rows, w_key, w_value, prompt_keys, prompt_values, swapped_out
):
    rows = pick(plan, gen_ids, embed_rows)
    places, beyond = find_places(plan, rows, gen_ids, embed_rows.shape[0])
    rest = lax.cond(
        beyond[0, 0] > 0.5,
        lambda: rows_beyond(plan, gen_ids, embed_rows),
        lambda: jnp.zeros((plan.tokens, plan.features), BF16),
    )
    w_key = bring(rest, w_key)
    across = [plan.over_head(rows, step * plan.inner) for step in range(1, plan.outer)]
    near = jnp.concatenate([rows, *across])
    near, w_key, swapped_out = lax.optimization_barrier((near, w_key, swapped_out))
    given = prompt_to_swap(plan, near, prompt_keys, prompt_values)
    w_value = bring(near, w_value)
    blocks = [near] + [plan.over_head(near, step) for step in range(1, plan.inner)[::-1]]
    size = plan.outer * plan.room

    def kernel(places_ref, beyond_ref, rest_ref, *refs):
        blocks, (out_ref, held, added, sem) = refs[: plan.inner], refs[plan.inner :]
        for block, ref in enumerate(blocks):
            held[block * size : (block + 1) * size] = ref[...]
        placed = jnp.dot(places_ref[...], held[...], preferred_element_type=F32)
        out_ref[...] = placed.astype(BF16)

        @pl.when(jnp.max(beyond_ref[...]) > 0.5)
        def _():
            copy = pltpu.make_async_copy(rest_ref, added, sem)
            copy.start()
            copy.wait()
            out_ref[...] = out_ref[...] + added[...]

    embedded = call(
        kernel,
        jax.ShapeDtypeStruct((plan.tokens, plan.features), BF16),
        [VMEM_SPEC] * 2 + [ANY_SPEC] + [VMEM_SPEC] * plan.inner,
        VMEM_SPEC,
        [
            pltpu.VMEM((plan.inner * size, plan.features), BF16),
            pltpu.VMEM((plan.tokens, plan.features), BF16),
            pltpu.SemaphoreType.DMA,
        ],
        16,
        places,
        beyond,
        rest,
        *blocks,
    )
    return embedded, w_key, w_value, given, swapped_out


def prompt_half(plan, prompt_keys, prompt_values, after):
    rows, half = plan.prompt_rows, plan.half

    def kernel(_, keys_ref, values_ref, out_ref, sems):
        window = aligned(lax.rem(lax.axis_index("seq"), CORES), half)
        copies = [
            pltpu.make_async_copy(
                source.at[:, window], out_ref.at[pl.ds(place * rows, rows)], sems.at[place]
            )
            for place, source in enumerate((keys_ref, values_ref))
        ]
        for copy in copies:
            copy.start()
        for copy in copies:
            copy.wait()

    return call(
        kernel,
        jax.ShapeDtypeStruct((2 * rows, half), BF16),
        [ANY_SPEC] * 3,
        ANY_SPEC,
        [pltpu.SemaphoreType.DMA((2,))],
        4,
        after,
        in_hbm(prompt_keys),
        in_hbm(prompt_values),
    )


def project_half(plan, embedded, weights, other, dtype):
    half = plan.half

    def kernel(rows_ref, *refs):
        sources, out_ref = refs[:3], refs[3]
        core = lax.rem(lax.axis_index("seq"), CORES)
        window = aligned(1 - core if other else core, half)
        for kind in range(3):
            product = jnp.dot(
                rows_ref[...], sources[kind][:, window], preferred_element_type=F32
            )
            out_ref[:, kind * half : (kind + 1) * half] = product.astype(dtype)

    return call(
        kernel,
        jax.ShapeDtypeStruct((plan.tokens, 3 * half), dtype),
        [VMEM_SPEC] * 4,
        VMEM_SPEC,
        [],
        16,
        embedded,
        *weights,
    )


def sum_cores(plan, own, received):
    tokens, half, owned = plan.tokens, plan.half, plan.owned

    def kernel(own_ref, received_ref, *refs):
        outs, total = refs[: plan.chips], refs[plan.chips]
        total[...] = own_ref[...] + received_ref[...].astype(F32)
        chip = lax.axis_index("seq") // CORES
        for dy in range(plan.chips):
            out, rows = outs[dy], aligned(chip ^ dy, owned)
            out[:tokens] = total[:, :half].astype(out.dtype)
            out[tokens : tokens + owned] = total[rows, half : 2 * half].astype(out.dtype)
            out[tokens + owned :] = total[rows, 2 * half :].astype(out.dtype)

    shape = (tokens + 2 * owned, half)
    return call(
        kernel,
        [jax.ShapeDtypeStruct(shape, BF16 if dy else F32) for dy in range(plan.chips)],
        [VMEM_SPEC] * 2,
        [VMEM_SPEC] * plan.chips,
        [pltpu.VMEM((tokens, 3 * half), F32)],
        8,
        own,
        received,
    )


def project(plan, embedded, weights):
    received = plan.over_seq(project_half(plan, embedded, weights, True, BF16), 1)
    own = project_half(plan, embedded, weights, False, F32)
    parts = sum_cores(plan, own, received)
    return [parts[0]] + [plan.over_seq(parts[dy], dy * CORES) for dy in range(1, plan.chips)]


def angle_tables(plan):
    half_size = HD // 2
    frequency = 10000.0 ** (-jnp.arange(half_size, dtype=F32) / half_size)
    positions = plan.prompt_rows * plan.seq + jnp.arange(plan.steps, dtype=jnp.int32)
    angles = positions.astype(F32)[:, None] * frequency[None, :]
    cosine, sine_part = jnp.cos(angles), jnp.sin(angles)
    return (
        jnp.concatenate([cosine, cosine], axis=-1),
        jnp.concatenate([-sine_part, sine_part], axis=-1),
    )


def attend(plan, parts, kept, swapped, tables):
    tokens, half, owned, share = plan.tokens, plan.half, plan.owned, plan.share
    rows = plan.prompt_rows
    scale = 1.0 / math.sqrt(HD)
    transposed = (((1,), (1,)), ((), ()))

    def kernel(*refs):
        sums, refs = refs[: plan.chips], refs[plan.chips :]
        kept_ref, keys_ref, values_ref, cosine_ref, sine_ref = refs[:5]
        near_ref, far_ref, result = refs[5:]
        core = lax.rem(lax.axis_index("seq"), CORES)
        chip = lax.axis_index("seq") // CORES
        total = sums[0][...]
        for dy in range(1, plan.chips):
            total = total + sums[dy][...].astype(F32)
        cosine, sine_part = cosine_ref[...][None], sine_ref[...][None]

        def rotated(vectors):
            turned = pltpu.roll(vectors, HD // 2, 1)
            shaped = vectors.reshape(-1, plan.steps, HD) * cosine
            shaped = shaped + turned.reshape(-1, plan.steps, HD) * sine_part
            return shaped.reshape(vectors.shape).astype(BF16)

        pair = 2 * HD
        row = lax.broadcasted_iota(jnp.int32, (2 * tokens, 2 * owned), 0)
        column = lax.broadcasted_iota(jnp.int32, (2 * tokens, 2 * owned), 1)
        same_head = row // tokens == column // owned
        row, column = lax.rem(row, tokens), lax.rem(column, owned) + chip * owned
        seen = same_head & (row // plan.steps == column // plan.steps) & (column <= row)
        lane = lax.broadcasted_iota(jnp.int32, (tokens, HD), 1)
        logs = jnp.zeros((tokens, HD), F32)
        nothing = jnp.zeros((tokens, HD), BF16)
        for start in range(0, half, pair):
            lanes = slice(start, start + pair)
            near, far = slice(start, start + HD), slice(start + HD, start + pair)
            query = jnp.concatenate(
                [
                    jnp.concatenate([rotated(total[:tokens, near]), nothing], axis=1),
                    jnp.concatenate([nothing, rotated(total[:tokens, far])], axis=1),
                ]
            )
            keys, values = slice(tokens, tokens + owned), slice(tokens + owned, None)
            gen_key = jnp.concatenate([rotated(total[keys, near]), rotated(total[keys, far])])
            gen_value = jnp.concatenate([total[values, near], total[values, far]]).astype(BF16)

            def score(vectors, key):
                return (
                    lax.dot_general(vectors, key, transposed, preferred_element_type=F32) * scale
                )

            own = score(jnp.concatenate([query[:tokens, :HD], query[tokens:, HD:]]), gen_key)
            scores = [
                score(query, kept_ref[:rows, lanes]),
                score(query, keys_ref[:, lanes]),
                jnp.where(seen, own, -jnp.inf),
            ]
            peak = jnp.max(scores[0], axis=1, keepdims=True)
            for part in scores[1:]:
                peak = jnp.maximum(peak, jnp.max(part, axis=1, keepdims=True))
            weights = [jnp.exp(part - peak) for part in scores]
            weight_sum = sum(jnp.sum(weight, axis=1, keepdims=True) for weight in weights)
            weights = [weight.astype(BF16) for weight in weights]
            summed = jnp.dot(
                weights[0], kept_ref[rows:, lanes], preferred_element_type=F32
            ) + jnp.dot(weights[1], values_ref[:, lanes], preferred_element_type=F32)
            summed = jnp.concatenate([summed[:tokens, :HD], summed[tokens:, HD:]])
            summed = summed + jnp.dot(weights[2], gen_value, preferred_element_type=F32)
            mixed = (summed / weight_sum).astype(BF16)
            result[:, near] = mixed[:tokens]
            result[:, far] = mixed[tokens:]
            both = peak + jnp.log(weight_sum)
            for place, rest in enumerate((both[:tokens], both[tokens:])):
                first = 3 * (start // HD + place)
                for term in range(3):
                    piece = rest.astype(BF16).astype(F32)
                    rest = rest - piece
                    logs = jnp.where(lane == first + term, piece, logs)
        result[:, half:] = logs.astype(BF16)
        for pair in range(plan.chips):
            place = pl.ds(pair * share, share)
            near_ref[place, :] = result[aligned(pair * CORES + core, share), :]
            far_ref[place, :] = result[aligned(pair * CORES + 1 - core, share), :]

    out = jax.ShapeDtypeStruct((tokens // CORES, half + HD), BF16)
    near, far = call(
        kernel,
        [out] * 2,
        [VMEM_SPEC] * (plan.chips + 5),
        [VMEM_SPEC] * 2,
        [pltpu.VMEM((tokens, half + HD), BF16)],
        24,
        *parts,
        kept,
        *swapped,
        *tables,
    )
    got = {k: plan.over_seq(far if k % CORES else near, k) for k in range(1, plan.seq)}
    return [near] + [got[k] for k in range(1, plan.seq)]


def multiply_out(plan, attended, own, swapped):
    share, half, columns = plan.share, plan.half, plan.columns
    rows = plan.tokens // CORES
    keys = [(dy, dx) for dx in range(plan.parts) for dy in range(plan.chips)]

    def kernel(*refs):
        parts, refs = refs[: plan.seq], refs[plan.seq :]
        (own_ref, swapped_ref), refs = refs[:2], refs[2:]
        outs, (joined,) = refs[: len(keys)], refs[len(keys) :]
        seq_index = lax.axis_index("seq")
        chip, core = seq_index // CORES, lax.rem(seq_index, CORES)
        part_index = lax.rem(lax.axis_index("head"), plan.parts)
        for side in range(CORES):
            sources = [parts[step] for step in range(side, plan.seq, CORES)]
            first = (core ^ side) * half
            for head in range(half // HD):
                lanes = slice(head * HD, (head + 1) * HD)
                logs = [
                    sum(
                        source[:, half + 3 * head + term : half + 3 * head + term + 1].astype(F32)
                        for term in (2, 1, 0)
                    )
                    for source in sources
                ]
                top = logs[0]
                for one in logs[1:]:
                    top = jnp.maximum(top, one)
                scales = [jnp.exp(one - top) for one in logs]
                mixed = sum(f * source[:, lanes].astype(F32) for f, source in zip(scales, sources))
                mixed = (mixed / sum(scales)).astype(BF16)
                window = pl.ds(pl.multiple_of(first + head * HD, HD), HD)
                for owner in range(plan.chips):
                    rows_of = mixed[owner * share : (owner + 1) * share]
                    joined[aligned(owner ^ chip, share), window] = rows_of
        left = joined[...]
        for dx in list(range(plan.parts))[::-1]:
            lanes = aligned(part_index ^ dx, columns)
            for weight, block in ((own_ref, core), (swapped_ref, 1 - core)):
                product = jnp.dot(left, weight[:, lanes], preferred_element_type=F32)
                for dy in range(plan.chips):
                    out = outs[keys.index((dy, dx))]
                    out[block] = product[dy * share : (dy + 1) * share].astype(out.dtype)

    shape = (CORES, share, columns)
    outs = [jax.ShapeDtypeStruct(shape, BF16 if any(key) else F32) for key in keys]
    made = call(
        kernel,
        outs,
        [VMEM_SPEC] * (plan.seq + 2),
        [VMEM_SPEC] * len(keys),
        [pltpu.VMEM((rows, plan.width), BF16)],
        24,
        *attended,
        own,
        swapped,
    )
    got = {}
    for key, value in list(zip(keys, made))[::-1]:
        dy, dx = key
        if any(key):
            value = plan.send(value, lambda s, h: (s ^ (dy * CORES), h ^ dx))
        got[key] = value
    return got


def sum_parts(plan, got):
    keys = list(got)
    shape = (plan.share, plan.columns)

    def kernel(*refs):
        ins, refs = dict(zip(keys, refs)), refs[len(keys) :]
        outs, (held,) = refs[: plan.seq], refs[plan.seq :]
        chip = lax.axis_index("seq") // CORES
        place = lax.axis_index("head") // plan.parts
        for dy in range(plan.chips):
            total = ins[dy, 0][...].astype(F32)
            for dx in range(1, plan.parts):
                total = total + ins[dy, dx][...].astype(F32)
            for core in range(CORES):
                held[(chip ^ dy) * CORES + core] = total[core]
        for step in range(plan.seq):
            outs[step][...] = held[place ^ step].astype(outs[step].dtype)

    outs = [jax.ShapeDtypeStruct(shape, BF16 if step else F32) for step in range(plan.seq)]
    made = call(
        kernel,
        outs,
        [VMEM_SPEC] * len(keys),
        [VMEM_SPEC] * plan.seq,
        [pltpu.VMEM((plan.seq,) + shape, F32)],
        16,
        *got.values(),
    )
    got = [
        plan.send(made[step], lambda s, h: (s, h ^ (step * plan.parts)))
        for step in list(range(1, plan.seq))[::-1]
    ]

    def last(*refs):
        total = refs[0][...]
        for ref in refs[1:-1]:
            total = total + ref[...].astype(F32)
        refs[-1][...] = total.astype(BF16)

    return call(
        last,
        jax.ShapeDtypeStruct(shape, BF16),
        [VMEM_SPEC] * plan.seq,
        VMEM_SPEC,
        [],
        8,
        made[0],
        *got,
    )


def solution(mesh):
    def body(gen_ids, embed_rows, w_query, w_key, w_value, w_out, prompt_keys, prompt_values):
        plan = Plan(mesh, gen_ids, w_query, w_out, prompt_keys)
        swapped_out = plan.over_seq(w_out, 1)
        embedded, w_key, w_value, given, swapped_out = gather_embedded(
            plan, gen_ids, embed_rows, w_key, w_value, prompt_keys, prompt_values, swapped_out
        )
        swapped = [plan.over_seq(part, 1) for part in given]
        parts = project(plan, embedded, (w_query, w_key, w_value))
        kept = prompt_half(plan, prompt_keys, prompt_values, parts[0])
        swapped_out = bring(parts[0], swapped_out)
        attended = attend(plan, parts, kept, swapped, angle_tables(plan))
        return sum_parts(plan, multiply_out(plan, attended, w_out, swapped_out))

    return jax.shard_map(
        body,
        mesh=mesh,
        in_specs=(
            P(),
            P("head", "seq"),
            P("seq", "head"),
            P("seq", "head"),
            P("seq", "head"),
            P("head", "seq"),
            P("seq", "head"),
            P("seq", "head"),
        ),
        out_specs=P("seq", "head"),
        check_vma=False,
    )
```
